32 devices in a mesh: hi: 8 (over z, y), lo: 4 (over x, core).
Axes of the slice: x: 2, y: 2, z: 4, core: 2. Of those that a mesh axis runs over, the one named last changes fastest.
Arguments:
- amplitudes: float32 [2, 32, 512, 256], P(None, ('hi', 'lo')), may hold values from -6 to 6
- joined_gates: float32 [2, 2, 512, 512], replicated, may hold values from -0.1875 to 0.1875
- pair_gates: float32 [2, 2, 2, 2], replicated, may hold values from -3 to 3
- global_angles: float32 [2, 32], P(None, ('hi', 'lo')), may hold values from -3.140625 to 3.140625
- local_phases: float32 [2, 17], replicated, may hold values from -3.140625 to 3.140625
- slice_bits: int32 [17], replicated, may hold values from 0 to 1
- coupled_qubits: int32 [2, 17], replicated, may hold values from 0 to 16
- gate_layout: int32 [9], replicated, may hold values from 0 to 8, each once
Outputs:
- evolved: float32 [2, 32, 512, 256], P(None, ('hi', 'lo'))
The draws below stay inside these ranges and needn't reach their ends.
Inputs may be any that keep to these rules, and one draw needn't show every extreme that they name: `gate_layout`: each of 0 to 8 once.
All inputs are finite; a program needn't handle non-finite values.
Results may differ from the reference program's by a relative error of at most 0.0001.
Values sent between devices are 32-bit elements; how exact they have to be, the bound alone decides.
No kernel may reach another device: no remote copies, remote signals or barrier semaphores. Data moves between devices by JAX's collectives and lax.ppermute only.
A program may use at most 64 MiB of HBM per device.

```python
import math
import jax
import jax.numpy as jnp
from jax import lax

ROW_BITS = 9
COL_BITS = 8
FIXED = 17
LAYERS = 2
ROWS = 512
COLS = 256
LQ = 17
N_HI = 8
N_LO = 4
DEVICES = 32


def touch_ends(entries, rng, least, top_value):
    dims = entries.shape
    spot = [jax.random.randint(jax.random.fold_in(rng, axis), (), 0, dims[axis]) for axis in range(len(dims))]
    entries = entries.at[tuple(spot)].set(least)
    longest = dims.index(max(dims))
    spot[longest] = (spot[longest] + 1) % dims[longest]
    return entries.at[tuple(spot)].set(top_value)


def block_levels(own_key, dims, shards, low, top_value):
    def one(dim, parts):
        heights = jax.random.uniform(jax.random.fold_in(jax.random.fold_in(own_key, 6), dim), (parts,), jnp.float32, low / len(shards), top_value / len(shards))
        return jnp.repeat(jnp.exp(heights), dims[dim] // parts).reshape((-1,) + (1,) * (len(dims) - dim - 1))

    factor_of = one(*shards[0])
    for cut in shards[1:]:
        factor_of = factor_of * one(*cut)
    return factor_of


def bell_draw(key, dims, scale, limit, split=(), kind=jnp.bfloat16):
    factor_of = block_levels(key, dims, split, -0.22, 0.18) if split else 1.0
    entries = jax.random.normal(key, dims, jnp.float32) * scale * factor_of
    return jnp.minimum(jnp.maximum(entries, -limit), limit).astype(kind)


def setup_inputs(seed: int = 0) -> dict:
    key_of = jax.random.split(jax.random.key(seed), 9)
    return {
        "amplitudes": bell_draw(key_of[0], (2, DEVICES, ROWS, COLS), 1.0, 6.0, ((1, 32),), jnp.float32),
        "joined_gates": bell_draw(key_of[1], (LAYERS, 2, ROWS, ROWS), (2 * ROWS) ** -0.5, 0.1875, (), jnp.float32),
        "pair_gates": bell_draw(key_of[2], (LAYERS, 2, 2, 2), 0.5, 3.0, (), jnp.float32),
        "global_angles": jnp.clip(jax.random.uniform(key_of[3], (LAYERS, DEVICES), jnp.float32, -3.140625, 3.140625), -3.140625, 3.140625),
        "local_phases": jnp.clip(jax.random.uniform(key_of[4], (LAYERS, LQ), jnp.float32, -3.140625, 3.140625), -3.140625, 3.140625),
        "slice_bits": touch_ends(jax.random.randint(key_of[5], (FIXED,), 0, 2), jax.random.fold_in(key_of[5], 1), 0, 1).astype(jnp.int32),
        "coupled_qubits": touch_ends(jax.random.randint(key_of[6], (LAYERS, FIXED), 0, LQ), jax.random.fold_in(key_of[6], 1), 0, LQ - 1).astype(jnp.int32),
        "gate_layout": jax.random.permutation(key_of[7], ROW_BITS).astype(jnp.int32),
    }


def bit_angles(angles, bit_count, length):
    positions = jnp.arange(length, dtype=jnp.int32)
    summed = jnp.zeros((length,), jnp.float32)
    for bit_pos in range(bit_count):
        chosen = ((positions >> bit_pos) & 1).astype(jnp.float32)
        summed = summed + chosen * angles[bit_pos]
    return summed


def qubit_angles(local_phases, slice_bits, coupled_qubits, layer_id):
    qubits = jnp.arange(LQ, dtype=jnp.int32)
    matches = (coupled_qubits[layer_id][:, None] == qubits[None, :]).astype(jnp.float32)
    flipped = jnp.sum(matches * slice_bits[:, None].astype(jnp.float32), axis=0)
    return local_phases[layer_id] + math.pi * flipped


def folded_gate(joined_gates, layer_id, device_angle, row_angles):
    turned = row_angles + device_angle
    cosine = jnp.cos(turned)[None, :]
    sine = jnp.sin(turned)[None, :]
    gate_real = joined_gates[layer_id, 0]
    gate_imag = joined_gates[layer_id, 1]
    return gate_real * cosine - gate_imag * sine, gate_real * sine + gate_imag * cosine


def gate_block(block, weight_real, weight_imag, col_angles):
    precise = lax.Precision.HIGHEST
    real_real = jnp.dot(weight_real, block[0], precision=precise, preferred_element_type=jnp.float32)
    real_imag = jnp.dot(weight_real, block[1], precision=precise, preferred_element_type=jnp.float32)
    imag_real = jnp.dot(weight_imag, block[0], precision=precise, preferred_element_type=jnp.float32)
    imag_imag = jnp.dot(weight_imag, block[1], precision=precise, preferred_element_type=jnp.float32)
    new_real = real_real - imag_imag
    new_imag = real_imag + imag_real
    cosine = jnp.cos(col_angles)[None, :]
    sine = jnp.sin(col_angles)[None, :]
    return jnp.stack([new_real * cosine - new_imag * sine, new_real * sine + new_imag * cosine])


def local_layer(blocks, joined_gates, global_angles, angles, layer_id):
    row_angles = bit_angles(angles[COL_BITS:], ROW_BITS, ROWS)
    col_angles = bit_angles(angles, COL_BITS, COLS)

    def one_device(pieces):
        block, device_angle = pieces
        weight_real, weight_imag = folded_gate(joined_gates, layer_id, device_angle, row_angles)
        return gate_block(block, weight_real, weight_imag, col_angles)

    return lax.map(one_device, (blocks, global_angles[layer_id]))


def pair_gate(blocks, pair_gates, layer_id, bit_pos):
    stride = 2 ** bit_pos
    shaped = blocks.reshape(DEVICES // (2 * stride), 2, stride, 2, ROWS, COLS)
    lower = shaped[:, 0]
    upper = shaped[:, 1]
    coeff_real = pair_gates[layer_id, 0]
    coeff_imag = pair_gates[layer_id, 1]
    outputs = []
    for side in range(2):
        new_real = (coeff_real[side, 0] * lower[:, :, 0] - coeff_imag[side, 0] * lower[:, :, 1]
                    + coeff_real[side, 1] * upper[:, :, 0] - coeff_imag[side, 1] * upper[:, :, 1])
        new_imag = (coeff_real[side, 0] * lower[:, :, 1] + coeff_imag[side, 0] * lower[:, :, 0]
                    + coeff_real[side, 1] * upper[:, :, 1] + coeff_imag[side, 1] * upper[:, :, 0])
        outputs.append(jnp.stack([new_real, new_imag], axis=2))
    return jnp.stack(outputs, axis=1).reshape(DEVICES, 2, ROWS, COLS)


def row_order(gate_layout):
    positions = jnp.arange(ROWS, dtype=jnp.int32)
    source = jnp.zeros((ROWS,), jnp.int32)
    for bit_pos in range(ROW_BITS):
        place = jnp.left_shift(jnp.ones((), jnp.int32), gate_layout[bit_pos].astype(jnp.int32))
        source = source + ((positions >> bit_pos) & 1) * place
    return source.astype(jnp.int32)


def remap(blocks, gate_layout):
    permuted = jnp.take(blocks, row_order(gate_layout), axis=2)
    shaped = permuted.reshape(N_HI, N_LO, 2, N_HI, ROWS // N_HI, COLS)
    return jnp.swapaxes(shaped, 0, 3).reshape(DEVICES, 2, ROWS, COLS)


def reference(amplitudes, joined_gates, pair_gates, global_angles, local_phases, slice_bits, coupled_qubits, gate_layout):
    blocks = jnp.moveaxis(amplitudes, 1, 0)
    top_bit = N_LO.bit_length() - 2
    for layer_id in range(LAYERS):
        angles = qubit_angles(local_phases, slice_bits, coupled_qubits, layer_id)
        blocks = local_layer(blocks, joined_gates, global_angles, angles, layer_id)
        blocks = pair_gate(blocks, pair_gates, layer_id, top_bit if layer_id % 2 == 0 else 0)
        if layer_id + 1 < LAYERS:
            blocks = remap(blocks, gate_layout)
    return jnp.moveaxis(blocks, 0, 1)
```

```python
import functools

import jax
import jax.numpy as jnp
from jax import lax
from jax.experimental import pallas as pl
from jax.experimental.pallas import tpu as pltpu
from jax.sharding import PartitionSpec as P

F32 = jnp.float32
BF16 = jnp.bfloat16
VMEM_BYTES = 32 * 1024 * 1024


def sincos(x):
    turns = jnp.floor(x * 0.6366197723675814 + 0.5)
    r = x - turns * 1.5703125
    r = r - turns * 4.837512969970703125e-4
    r = r - turns * 7.54978995489188216e-8
    z = r * r
    sine = r + r * z * ((-1.9515295891e-4 * z + 8.3321608736e-3) * z - 1.6666654611e-1)
    cosine = 1.0 - 0.5 * z + z * z * (
        (2.443315711809948e-5 * z - 1.388731625493765e-3) * z + 4.166664568298827e-2
    )
    quarter = turns.astype(jnp.int32) & 3
    odd = (quarter & 1) == 1
    new_sine = jnp.where(odd, cosine, sine)
    new_cosine = jnp.where(odd, sine, cosine)
    new_sine = jnp.where((quarter & 2) == 2, -new_sine, new_sine)
    new_cosine = jnp.where(((quarter + 1) & 2) == 2, -new_cosine, new_cosine)
    return new_cosine, new_sine


def qubit_factors(layer, phases_ref, bits_ref, coupled_ref):
    qubits = phases_ref.shape[1]
    lane = lax.broadcasted_iota(jnp.int32, (1, qubits), 1)
    odd = jnp.zeros((1, qubits), jnp.int32)
    for f in range(bits_ref.shape[0]):
        odd = odd ^ jnp.where(lane == coupled_ref[layer, f], bits_ref[f], 0)
    sign = 1.0 - 2.0 * odd.astype(F32)
    cosine, sine = sincos(phases_ref[layer : layer + 1, :])
    return cosine * sign, sine * sign


def turn(real, imag, cosine, sine):
    return real * cosine - imag * sine, real * sine + imag * cosine


def row_phases(cosine, sine, first, row_bits, base_real, base_imag):
    sub = lax.broadcasted_iota(jnp.int32, (8, 128), 0)
    real = jnp.broadcast_to(base_real, (8, 128))
    imag = jnp.broadcast_to(base_imag, (8, 128))
    for k in range(row_bits):
        c = cosine[:, first + k : first + k + 1]
        s = sine[:, first + k : first + k + 1]
        if k < 3:
            chosen = ((sub >> k) & 1) == 1
            real, imag = turn(real, imag, jnp.where(chosen, c, 1.0), jnp.where(chosen, s, 0.0))
        else:
            up_real, up_imag = turn(real, imag, c, s)
            real = jnp.concatenate([real, up_real], axis=0)
            imag = jnp.concatenate([imag, up_imag], axis=0)
    return real, imag


def col_phases(cosine, sine, col_bits, cols):
    lane = lax.broadcasted_iota(jnp.int32, (1, cols), 1)
    real = jnp.ones((1, cols), F32)
    imag = jnp.zeros((1, cols), F32)
    for k in range(col_bits):
        chosen = ((lane >> k) & 1) == 1
        c = cosine[:, k : k + 1]
        s = sine[:, k : k + 1]
        real, imag = turn(real, imag, jnp.where(chosen, c, 1.0), jnp.where(chosen, s, 0.0))
    return real, imag


def split(x):
    high = x.astype(BF16)
    low = (x - high.astype(F32)).astype(BF16)
    return high, low


def dot(a, b):
    return jnp.dot(a, b, preferred_element_type=F32)


def turned_rows(real, imag, phase_real, phase_imag):
    reps = real.shape[1] // phase_real.shape[1]
    phase_real = jnp.concatenate([phase_real] * reps, axis=1)
    phase_imag = jnp.concatenate([phase_imag] * reps, axis=1)
    real, imag = turn(real, imag, phase_real, phase_imag)
    real_high, real_low = split(real)
    imag_high, imag_low = split(imag)

    def block(r, i):
        return jnp.concatenate(
            [jnp.concatenate([r, i], axis=1), jnp.concatenate([-i, r], axis=1)], axis=0
        )

    return block(real_high, imag_high), block(real_low, imag_low)


def product(left_high, left_low, right_high, right_low):
    return dot(left_high, right_high) + dot(left_high, right_low) + dot(left_low, right_high)


def first_gate_kernel(
    groups,
    piece_rows,
    col_bits,
    amplitudes_ref,
    gates_ref,
    phases_ref,
    angles_ref,
    bits_ref,
    coupled_ref,
    layout_ref,
    *out_refs,
):
    me = lax.axis_index("hi")
    rows = amplitudes_ref.shape[2]
    cols = amplitudes_ref.shape[3]
    row_bits = rows.bit_length() - 1
    cosine, sine = qubit_factors(0, phases_ref, bits_ref, coupled_ref)
    base_real, base_imag = sincos(angles_ref[0:1, 0:1])
    phase_real, phase_imag = row_phases(cosine, sine, col_bits, row_bits, base_real, base_imag)
    right_high, right_low = turned_rows(
        amplitudes_ref[0, 0], amplitudes_ref[1, 0], phase_real, phase_imag
    )
    sub = lax.broadcasted_iota(jnp.int32, (8, 128), 0)
    inner = jnp.zeros((8, 128), jnp.int32)
    inner_bits = piece_rows.bit_length() - 1
    for k in range(inner_bits):
        place = jnp.left_shift(jnp.int32(1), layout_ref[k])
        if k < 3:
            inner = inner + ((sub >> k) & 1) * place
        else:
            inner = jnp.concatenate([inner, inner + place], axis=0)
    places = []
    for group in groups:
        for step in group:
            block = me ^ step
            base = jnp.int32(0)
            for k in range(inner_bits, row_bits):
                base = base + jnp.left_shift((block >> (k - inner_bits)) & 1, layout_ref[k])
            places.append(inner + base)
    places = jnp.concatenate(places, axis=0)
    lane = lax.broadcasted_iota(jnp.int32, places.shape, 1)
    chosen = jnp.concatenate(
        [
            jnp.where(places == lane + start, 1.0, 0.0).astype(BF16)
            for start in range(0, rows, 128)
        ],
        axis=1,
    )
    gate_real_high, gate_real_low = split(gates_ref[0, 0])
    gate_imag_high, gate_imag_low = split(gates_ref[0, 1])
    left_high = dot(chosen, jnp.concatenate([gate_real_high, gate_imag_high], axis=1)).astype(BF16)
    left_low = dot(chosen, jnp.concatenate([gate_real_low, gate_imag_low], axis=1)).astype(BF16)
    out = product(left_high, left_low, right_high, right_low)
    start = 0
    for group, out_ref in zip(groups, out_refs, strict=True):
        size = len(group) * piece_rows
        out_ref[0] = out[start : start + size, :cols]
        out_ref[1] = out[start : start + size, cols:]
        start += size


def smem():
    return pl.BlockSpec(memory_space=pltpu.SMEM)


def vmem():
    return pl.BlockSpec(memory_space=pltpu.VMEM)


def first_gate(groups, piece_rows, col_bits, amplitudes, gates, phases, angles, bits, coupled, layout):
    cols = amplitudes.shape[3]
    whole = lambda a: pl.BlockSpec(a.shape, lambda i: (0,) * a.ndim)
    shapes = [
        jax.ShapeDtypeStruct((2, len(group) * piece_rows, cols), F32) for group in groups
    ]
    return pl.pallas_call(
        functools.partial(first_gate_kernel, groups, piece_rows, col_bits),
        grid=(1,),
        out_shape=shapes,
        in_specs=[
            whole(amplitudes),
            pl.BlockSpec((1,) + gates.shape[1:], lambda i: (0, 0, 0, 0)),
            whole(phases),
            whole(angles),
            smem(),
            smem(),
            smem(),
        ],
        out_specs=[pl.BlockSpec(s.shape, lambda i: (0, 0, 0)) for s in shapes],
        compiler_params=pltpu.CompilerParams(vmem_limit_bytes=VMEM_BYTES),
        name="first_gate",
    )(amplitudes, gates, phases, angles, bits, coupled, layout)


def pair_coefficients(pair_ref, layer, bit):
    own = bit
    other = 1 - bit
    return (
        pair_ref[layer, 0, own, own],
        pair_ref[layer, 1, own, own],
        pair_ref[layer, 0, own, other],
        pair_ref[layer, 1, own, other],
    )


def combined(own, other, c):
    own_real, own_imag = turn(own[0], own[1], c[0], c[1])
    other_real, other_imag = turn(other[0], other[1], c[2], c[3])
    return own_real + other_real, own_imag + other_imag


def combine_kernel(top_bit, own_ref, other_ref, pair_ref, *out_refs):
    bit = (lax.axis_index("lo") >> top_bit) & 1
    c = pair_coefficients(pair_ref, 0, bit)
    size = out_refs[0].shape[1]
    for i, out_ref in enumerate(out_refs):
        rows = slice(i * size, (i + 1) * size)
        out_ref[0], out_ref[1] = combined(
            (own_ref[0, rows], own_ref[1, rows]), (other_ref[0, rows], other_ref[1, rows]), c
        )


def combine(top_bit, count, own, other, pair_gates):
    shape = (2, own.shape[1] // count, own.shape[2])
    return pl.pallas_call(
        functools.partial(combine_kernel, top_bit),
        out_shape=[jax.ShapeDtypeStruct(shape, F32)] * count,
        in_specs=[vmem(), vmem(), smem()],
        out_specs=[vmem()] * count,
        compiler_params=pltpu.CompilerParams(vmem_limit_bytes=VMEM_BYTES),
        name="combine",
    )(own, other, pair_gates)


def second_gate_kernel(
    exchanged,
    ready,
    piece_rows,
    col_bits,
    top_bit,
    gates_ref,
    phases_ref,
    angles_ref,
    bits_ref,
    coupled_ref,
    pair_ref,
    *refs,
):
    me = lax.axis_index("hi")
    bit = (lax.axis_index("lo") >> top_bit) & 1
    c = pair_coefficients(pair_ref, 0, bit)
    out_ref, real_ref, imag_ref = refs[-3:]
    rows, cols = real_ref.shape
    row_bits = rows.bit_length() - 1
    position = 0

    def place(step, real, imag):
        start = pl.multiple_of((me ^ step) * piece_rows, piece_rows)
        real_ref[pl.ds(start, piece_rows), :] = real
        imag_ref[pl.ds(start, piece_rows), :] = imag

    for group in exchanged:
        own_ref, other_ref = refs[position : position + 2]
        position += 2
        for i, step in enumerate(group):
            part = slice(i * piece_rows, (i + 1) * piece_rows)
            place(
                step,
                *combined(
                    (own_ref[0, part], own_ref[1, part]),
                    (other_ref[0, part], other_ref[1, part]),
                    c,
                ),
            )
    for step in ready:
        place(step, refs[position][0], refs[position][1])
        position += 1
    cosine, sine = qubit_factors(1, phases_ref, bits_ref, coupled_ref)
    base_real, base_imag = sincos(angles_ref[1:2, 0:1])
    phase_real, phase_imag = row_phases(cosine, sine, col_bits, row_bits, base_real, base_imag)
    right_high, right_low = turned_rows(real_ref[...], imag_ref[...], phase_real, phase_imag)
    gate_real_high, gate_real_low = split(gates_ref[0, 0])
    gate_imag_high, gate_imag_low = split(gates_ref[0, 1])
    out = product(
        jnp.concatenate([gate_real_high, gate_imag_high], axis=1),
        jnp.concatenate([gate_real_low, gate_imag_low], axis=1),
        right_high,
        right_low,
    )
    out_ref[0] = out[:, :cols]
    out_ref[1] = out[:, cols:]


def second_gate(
    exchanged, ready, piece_rows, col_bits, top_bit, gates, phases, angles, bits, coupled, pair, arrays
):
    rows = gates.shape[2]
    cols = arrays[0].shape[2]
    whole = lambda a: pl.BlockSpec(a.shape, lambda i: (0,) * a.ndim)
    return pl.pallas_call(
        functools.partial(second_gate_kernel, exchanged, ready, piece_rows, col_bits, top_bit),
        grid=(1,),
        out_shape=jax.ShapeDtypeStruct((2, rows, cols), F32),
        in_specs=[
            pl.BlockSpec((1,) + gates.shape[1:], lambda i: (1, 0, 0, 0)),
            whole(phases),
            whole(angles),
            smem(),
            smem(),
            smem(),
        ]
        + [whole(a) for a in arrays],
        out_specs=pl.BlockSpec((2, rows, cols), lambda i: (0, 0, 0)),
        scratch_shapes=[pltpu.VMEM((rows, cols), F32)] * 2,
        compiler_params=pltpu.CompilerParams(vmem_limit_bytes=VMEM_BYTES),
        name="second_gate",
    )(gates, phases, angles, bits, coupled, pair, *arrays)


def last_kernel(col_bits, own_ref, other_ref, phases_ref, bits_ref, coupled_ref, pair_ref, out_ref):
    bit = lax.axis_index("lo") & 1
    cols = own_ref.shape[2]
    first_real, first_imag = col_phases(
        *qubit_factors(0, phases_ref, bits_ref, coupled_ref), col_bits, cols
    )
    second_real, second_imag = col_phases(
        *qubit_factors(1, phases_ref, bits_ref, coupled_ref), col_bits, cols
    )
    phase_real, phase_imag = turn(first_real, first_imag, second_real, second_imag)
    c = pair_coefficients(pair_ref, 1, bit)
    c = turn(phase_real, phase_imag, c[0], c[1]) + turn(phase_real, phase_imag, c[2], c[3])
    out_ref[0, 0], out_ref[1, 0] = combined(own_ref, other_ref, c)


def last(col_bits, own, other, phases, bits, coupled, pair):
    rows, cols = own.shape[1:]
    return pl.pallas_call(
        functools.partial(last_kernel, col_bits),
        out_shape=jax.ShapeDtypeStruct((2, 1, rows, cols), F32),
        in_specs=[vmem(), vmem(), vmem(), smem(), smem(), smem()],
        out_specs=vmem(),
        compiler_params=pltpu.CompilerParams(vmem_limit_bytes=VMEM_BYTES),
        name="last",
    )(own, other, phases, bits, coupled, pair)


def swap(value, axis, mask):
    return lax.ppermute(value, axis, [(i, i ^ mask) for i in range(lax.axis_size(axis))])


def shards(amplitudes, gates, pair, angles, phases, bits, coupled, layout):
    rows = amplitudes.shape[2]
    cols = amplitudes.shape[3]
    col_bits = cols.bit_length() - 1
    count = lax.axis_size("hi")
    piece_rows = rows // count
    top_bit = lax.axis_size("lo").bit_length() - 2
    quarter = count // 4
    near = tuple(range(1, 2 * quarter))
    far = tuple(range(2 * quarter, 3 * quarter))
    early = tuple(range(3 * quarter, count))
    first = functools.partial(
        first_gate,
        piece_rows=piece_rows,
        col_bits=col_bits,
        amplitudes=amplitudes,
        gates=gates,
        phases=phases,
        angles=angles,
        bits=bits,
        coupled=coupled,
        layout=layout,
    )
    cross = functools.partial(swap, axis="lo", mask=1 << top_bit)
    *far_parts, early_part = first(tuple((d,) for d in far) + (early,))
    far_parts = [swap(part, "hi", d) for part, d in zip(far_parts, far, strict=True)]
    early_other = cross(early_part)
    own_part, *near_parts = first(((0,),) + tuple((d,) for d in near))
    early_parts = combine(top_bit, len(early), early_part, early_other, pair)
    early_parts = [swap(part, "hi", d) for part, d in zip(early_parts, early, strict=True)]
    near_parts = [swap(part, "hi", d) for part, d in zip(near_parts, near, strict=True)]
    own_other = cross(own_part)
    near_part = jnp.concatenate(near_parts, axis=1)
    near_other = cross(near_part)
    far_part = jnp.concatenate(far_parts, axis=1)
    far_other = cross(far_part)
    gated = second_gate(
        ((0,), near, far),
        early,
        piece_rows,
        col_bits,
        top_bit,
        gates,
        phases,
        angles,
        bits,
        coupled,
        pair,
        [own_part, own_other, near_part, near_other, far_part, far_other, *early_parts],
    )
    return last(col_bits, gated, swap(gated, "lo", 1), phases, bits, coupled, pair)


def solution(mesh):
    placed = (
        P(None, ("hi", "lo"), None, None),
        P(),
        P(),
        P(None, ("hi", "lo")),
        P(),
        P(),
        P(),
        P(),
    )
    return jax.shard_map(
        shards,
        mesh=mesh,
        in_specs=placed,
        out_specs=P(None, ("hi", "lo"), None, None),
        check_vma=False,
    )
```

```python
import functools

import jax
import jax.numpy as jnp
from jax import lax
from jax.experimental import pallas as pl
from jax.experimental.pallas import tpu as pltpu
from jax.sharding import PartitionSpec as P

F32 = jnp.float32
BF16 = jnp.bfloat16
VMEM_BYTES = 32 * 1024 * 1024
MIDDLE_COST = 3000000000
HALF_COST = 1000
READY_COST = 1500001000
LATE_COST = 1000


def sincos(x):
    turns = jnp.floor(x * 0.6366197723675814 + 0.5)
    r = x - turns * 1.5703125
    r = r - turns * 4.837512969970703125e-4
    r = r - turns * 7.54978995489188216e-8
    z = r * r
    sine = r + r * z * ((-1.9515295891e-4 * z + 8.3321608736e-3) * z - 1.6666654611e-1)
    cosine = 1.0 - 0.5 * z + z * z * (
        (2.443315711809948e-5 * z - 1.388731625493765e-3) * z + 4.166664568298827e-2
    )
    quarter = turns.astype(jnp.int32) & 3
    odd = (quarter & 1) == 1
    new_sine = jnp.where(odd, cosine, sine)
    new_cosine = jnp.where(odd, sine, cosine)
    new_sine = jnp.where((quarter & 2) == 2, -new_sine, new_sine)
    new_cosine = jnp.where(((quarter + 1) & 2) == 2, -new_cosine, new_cosine)
    return new_cosine, new_sine


def qubit_factors(layer, phases_ref, bits_ref, coupled_ref):
    qubits = phases_ref.shape[1]
    lane = lax.broadcasted_iota(jnp.int32, (1, qubits), 1)
    odd = jnp.zeros((1, qubits), jnp.int32)
    for f in range(bits_ref.shape[0]):
        odd = odd ^ jnp.where(lane == coupled_ref[layer, f], bits_ref[f], 0)
    sign = 1.0 - 2.0 * odd.astype(F32)
    cosine, sine = sincos(phases_ref[layer : layer + 1, :])
    return cosine * sign, sine * sign


def turn(real, imag, cosine, sine):
    return real * cosine - imag * sine, real * sine + imag * cosine


def row_phases(cosine, sine, first, row_bits, base_real, base_imag):
    sub = lax.broadcasted_iota(jnp.int32, (8, 128), 0)
    real = jnp.broadcast_to(base_real, (8, 128))
    imag = jnp.broadcast_to(base_imag, (8, 128))
    for k in range(row_bits):
        c = cosine[:, first + k : first + k + 1]
        s = sine[:, first + k : first + k + 1]
        if k < 3:
            chosen = ((sub >> k) & 1) == 1
            real, imag = turn(real, imag, jnp.where(chosen, c, 1.0), jnp.where(chosen, s, 0.0))
        else:
            up_real, up_imag = turn(real, imag, c, s)
            real = jnp.concatenate([real, up_real], axis=0)
            imag = jnp.concatenate([imag, up_imag], axis=0)
    return real, imag


def col_phases(cosine, sine, col_bits, cols):
    lane = lax.broadcasted_iota(jnp.int32, (1, cols), 1)
    real = jnp.ones((1, cols), F32)
    imag = jnp.zeros((1, cols), F32)
    for k in range(col_bits):
        chosen = ((lane >> k) & 1) == 1
        c = cosine[:, k : k + 1]
        s = sine[:, k : k + 1]
        real, imag = turn(real, imag, jnp.where(chosen, c, 1.0), jnp.where(chosen, s, 0.0))
    return real, imag


def split(x):
    high = x.astype(BF16)
    low = (x - high.astype(F32)).astype(BF16)
    return high, low


def dot(a, b):
    return jnp.dot(a, b, preferred_element_type=F32)


def turned_rows(real, imag, phase_real, phase_imag):
    reps = real.shape[1] // phase_real.shape[1]
    phase_real = jnp.concatenate([phase_real] * reps, axis=1)
    phase_imag = jnp.concatenate([phase_imag] * reps, axis=1)
    real, imag = turn(real, imag, phase_real, phase_imag)
    real_high, real_low = split(real)
    imag_high, imag_low = split(imag)

    def block(r, i):
        return jnp.concatenate(
            [jnp.concatenate([r, i], axis=1), jnp.concatenate([-i, r], axis=1)], axis=0
        )

    return block(real_high, imag_high), block(real_low, imag_low)


def product(left_high, left_low, right_high, right_low):
    return dot(left_high, right_high) + dot(left_high, right_low) + dot(left_low, right_high)


def hbm(array):
    return pltpu.with_memory_space_constraint(array, pltpu.HBM)


def any_space():
    return pl.BlockSpec(memory_space=pl.ANY)


def smem():
    return pl.BlockSpec(memory_space=pltpu.SMEM)


def vmem():
    return pl.BlockSpec(memory_space=pltpu.VMEM)


def cost(flops=1000):
    return pl.CostEstimate(flops=flops, bytes_accessed=1000, transcendentals=0)


def params():
    return pltpu.CompilerParams(vmem_limit_bytes=VMEM_BYTES)


def chosen_rows(steps, piece_rows, rows, layout_ref):
    me = lax.axis_index("hi")
    row_bits = rows.bit_length() - 1
    sub = lax.broadcasted_iota(jnp.int32, (8, 128), 0)
    inner = jnp.zeros((8, 128), jnp.int32)
    inner_bits = piece_rows.bit_length() - 1
    for k in range(inner_bits):
        place = jnp.left_shift(jnp.int32(1), layout_ref[k])
        if k < 3:
            inner = inner + ((sub >> k) & 1) * place
        else:
            inner = jnp.concatenate([inner, inner + place], axis=0)
    places = []
    for step in steps:
        block = me ^ step
        base = jnp.int32(0)
        for k in range(inner_bits, row_bits):
            base = base + jnp.left_shift((block >> (k - inner_bits)) & 1, layout_ref[k])
        places.append(inner + base)
    places = jnp.concatenate(places, axis=0)
    lane = lax.broadcasted_iota(jnp.int32, places.shape, 1)
    return jnp.concatenate(
        [
            jnp.where(places == lane + start, 1.0, 0.0).astype(BF16)
            for start in range(0, rows, 128)
        ],
        axis=1,
    )


def gate_pieces(groups, piece_rows, layout_ref, gate_high, gate_low, right_high, right_low, out_refs):
    rows = gate_high.shape[0]
    cols = right_high.shape[1] // 2
    chosen = chosen_rows([d for group in groups for d in group], piece_rows, rows, layout_ref)
    left_high = dot(chosen, gate_high).astype(BF16)
    left_low = dot(chosen, gate_low).astype(BF16)
    out = product(left_high, left_low, right_high, right_low)
    start = 0
    for group, out_ref in zip(groups, out_refs, strict=True):
        size = len(group) * piece_rows
        out_ref[0] = out[start : start + size, :cols]
        out_ref[1] = out[start : start + size, cols:]
        start += size


def first_kernel(
    groups,
    piece_rows,
    col_bits,
    amplitudes_hbm,
    gates_hbm,
    phases_hbm,
    angles_hbm,
    bits_hbm,
    coupled_hbm,
    layout_hbm,
    *refs,
):
    (
        *out_refs,
        amplitudes_ref,
        gates_ref,
        phases_ref,
        angles_ref,
        bits_ref,
        coupled_ref,
        layout_ref,
        sems,
    ) = refs
    copies = [
        pltpu.make_async_copy(source, target, sems.at[i])
        for i, (source, target) in enumerate(
            (
                (phases_hbm, phases_ref),
                (angles_hbm, angles_ref),
                (bits_hbm, bits_ref),
                (coupled_hbm, coupled_ref),
                (layout_hbm, layout_ref),
                (gates_hbm.at[0, 0], gates_ref.at[0]),
                (gates_hbm.at[0, 1], gates_ref.at[1]),
                (amplitudes_hbm, amplitudes_ref),
            )
        )
    ]
    for copy in copies:
        copy.start()
    for copy in copies[:5]:
        copy.wait()
    rows = amplitudes_ref.shape[2]
    row_bits = rows.bit_length() - 1
    cosine, sine = qubit_factors(0, phases_ref, bits_ref, coupled_ref)
    base_real, base_imag = sincos(angles_ref[0:1, 0:1])
    phase_real, phase_imag = row_phases(cosine, sine, col_bits, row_bits, base_real, base_imag)
    high, low = [], []
    for i in range(2):
        copies[5 + i].wait()
        for parts, part in zip((high, low), split(gates_ref[i]), strict=True):
            parts.append(part)
    copies[7].wait()
    right_high, right_low = turned_rows(
        amplitudes_ref[0, 0], amplitudes_ref[1, 0], phase_real, phase_imag
    )
    gate_pieces(
        groups,
        piece_rows,
        layout_ref,
        jnp.concatenate(high, axis=1),
        jnp.concatenate(low, axis=1),
        right_high,
        right_low,
        out_refs,
    )


def first(groups, piece_rows, col_bits, amplitudes, gates, phases, angles, bits, coupled, layout):
    rows, cols = amplitudes.shape[2:]
    shapes = [jax.ShapeDtypeStruct((2, len(group) * piece_rows, cols), F32) for group in groups]
    sources = (amplitudes, gates, phases, angles, bits, coupled, layout)
    return pl.pallas_call(
        functools.partial(first_kernel, groups, piece_rows, col_bits),
        out_shape=shapes,
        in_specs=[any_space()] * len(sources),
        out_specs=[vmem()] * len(shapes),
        scratch_shapes=[
            pltpu.VMEM(amplitudes.shape, F32),
            pltpu.VMEM(gates.shape[1:], F32),
            pltpu.VMEM(phases.shape, F32),
            pltpu.VMEM(angles.shape, F32),
            pltpu.SMEM(bits.shape, jnp.int32),
            pltpu.SMEM(coupled.shape, jnp.int32),
            pltpu.SMEM(layout.shape, jnp.int32),
            pltpu.SemaphoreType.DMA((8,)),
        ],
        compiler_params=params(),
        cost_estimate=cost(),
        name="first",
    )(*[hbm(source) for source in sources])


def ready_kernel(
    col_bits, gates_hbm, phases_ref, angles_ref, bits_ref, coupled_ref, pair_ref, *refs
):
    (
        gate_high_ref,
        gate_low_ref,
        phase_real_ref,
        phase_imag_ref,
        coefficients_ref,
        gates_ref,
        sem,
    ) = refs
    copy = pltpu.make_async_copy(gates_hbm.at[1], gates_ref, sem)
    copy.start()
    rows = gates_ref.shape[1]
    cols = coefficients_ref.shape[1]
    row_bits = rows.bit_length() - 1
    bit = lax.axis_index("lo") & 1
    before = qubit_factors(0, phases_ref, bits_ref, coupled_ref)
    after = qubit_factors(1, phases_ref, bits_ref, coupled_ref)
    base_real, base_imag = sincos(angles_ref[0:1, 1:2])
    phase_real_ref[...], phase_imag_ref[...] = row_phases(
        *after, col_bits, row_bits, base_real, base_imag
    )
    phase_real, phase_imag = turn(
        *col_phases(*before, col_bits, cols), *col_phases(*after, col_bits, cols)
    )
    c = pair_coefficients(pair_ref, 1, bit)
    c = turn(phase_real, phase_imag, c[0], c[1]) + turn(phase_real, phase_imag, c[2], c[3])
    for i in range(4):
        coefficients_ref[i : i + 1, :] = c[i]
    coefficients_ref[4:8, :] = jnp.zeros((4, cols), F32)
    copy.wait()
    for i in range(2):
        high, low = split(gates_ref[i])
        gate_high_ref[:, i * rows : (i + 1) * rows] = high
        gate_low_ref[:, i * rows : (i + 1) * rows] = low


def ready(col_bits, gates, phases, angles, bits, coupled, pair):
    rows = gates.shape[2]
    cols = 1 << col_bits
    return pl.pallas_call(
        functools.partial(ready_kernel, col_bits),
        out_shape=[
            jax.ShapeDtypeStruct((rows, 2 * rows), BF16),
            jax.ShapeDtypeStruct((rows, 2 * rows), BF16),
            jax.ShapeDtypeStruct((rows, 128), F32),
            jax.ShapeDtypeStruct((rows, 128), F32),
            jax.ShapeDtypeStruct((8, cols), F32),
        ],
        in_specs=[any_space(), vmem(), vmem(), smem(), smem(), smem()],
        out_specs=[vmem()] * 5,
        scratch_shapes=[pltpu.VMEM(gates.shape[1:], F32), pltpu.SemaphoreType.DMA],
        compiler_params=params(),
        cost_estimate=cost(READY_COST),
        name="ready",
    )(hbm(gates), phases, angles, bits, coupled, pair)


def pair_coefficients(pair_ref, layer, bit):
    own = bit
    other = 1 - bit
    return (
        pair_ref[layer, 0, own, own],
        pair_ref[layer, 1, own, own],
        pair_ref[layer, 0, own, other],
        pair_ref[layer, 1, own, other],
    )


def combined(own, other, c):
    own_real, own_imag = turn(own[0], own[1], c[0], c[1])
    other_real, other_imag = turn(other[0], other[1], c[2], c[3])
    return own_real + other_real, own_imag + other_imag


def combine_kernel(top_bit, own_ref, other_ref, pair_ref, *out_refs):
    bit = (lax.axis_index("lo") >> top_bit) & 1
    c = pair_coefficients(pair_ref, 0, bit)
    size = out_refs[0].shape[1]
    for i, out_ref in enumerate(out_refs):
        rows = slice(i * size, (i + 1) * size)
        out_ref[0], out_ref[1] = combined(
            (own_ref[0, rows], own_ref[1, rows]), (other_ref[0, rows], other_ref[1, rows]), c
        )


def combine(top_bit, count, own, other, pair_gates):
    shape = (2, own.shape[1] // count, own.shape[2])
    return pl.pallas_call(
        functools.partial(combine_kernel, top_bit),
        out_shape=[jax.ShapeDtypeStruct(shape, F32)] * count,
        in_specs=[vmem(), vmem(), smem()],
        out_specs=[vmem()] * count,
        compiler_params=params(),
        cost_estimate=cost(),
        name="combine",
    )(own, other, pair_gates)


def partial_product(quarters, pieces, piece_rows, parts_refs, scratch_refs):
    gate_high_ref, gate_low_ref, phase_real_ref, phase_imag_ref = parts_refs
    real_ref, imag_ref = scratch_refs
    rows = gate_high_ref.shape[0]
    size = rows // 4
    quarter = size // piece_rows
    me = lax.axis_index("hi")
    for step, (real, imag) in pieces.items():
        offset = quarters.index(step // quarter) * size
        start = offset + ((me ^ step) & (quarter - 1)) * piece_rows
        start = pl.multiple_of(start, piece_rows)
        real_ref[pl.ds(start, piece_rows), :] = real
        imag_ref[pl.ds(start, piece_rows), :] = imag
    starts = [pl.multiple_of(((me // quarter) ^ q) * size, size) for q in quarters]

    def some_rows(ref):
        return jnp.concatenate([ref[pl.ds(start, size), :] for start in starts], axis=0)

    def some_cols(ref):
        shift = (0, rows)
        return jnp.concatenate(
            [
                ref[:, pl.ds(pl.multiple_of(start + extra, size), size)]
                for extra in shift
                for start in starts
            ],
            axis=1,
        )

    right_high, right_low = turned_rows(
        real_ref[...], imag_ref[...], some_rows(phase_real_ref), some_rows(phase_imag_ref)
    )
    out = product(some_cols(gate_high_ref), some_cols(gate_low_ref), right_high, right_low)
    cols = real_ref.shape[1]
    return out[:, :cols], out[:, cols:]


def late_kernel(*refs):
    *part_refs, out_ref = refs
    size = part_refs[0].shape[1]
    for i, part_ref in enumerate(part_refs):
        out_ref[:, i * size : (i + 1) * size, :] = part_ref[...]


def joined(arrays, flops):
    _, size, cols = arrays[0].shape
    return pl.pallas_call(
        late_kernel,
        out_shape=jax.ShapeDtypeStruct((2, size * len(arrays), cols), F32),
        in_specs=[vmem()] * len(arrays),
        out_specs=vmem(),
        compiler_params=params(),
        cost_estimate=cost(flops),
        name="joined",
    )(*arrays)


def split_pieces(ref, steps, piece_rows):
    pieces = {}
    for i, step in enumerate(steps):
        part = slice(i * piece_rows, (i + 1) * piece_rows)
        pieces[step] = (ref[0, part], ref[1, part])
    return pieces


def middle_kernel(quarters, landed, piece_rows, *refs):
    landed_refs = refs[4:-3]
    out_ref = refs[-3]
    pieces = {step: (ref[0], ref[1]) for step, ref in zip(landed, landed_refs, strict=True)}
    out_ref[0], out_ref[1] = partial_product(quarters, pieces, piece_rows, refs[:4], refs[-2:])


def middle(quarters, landed, piece_rows, parts, arrays):
    rows = parts[0].shape[0]
    cols = arrays[0].shape[2]
    return pl.pallas_call(
        functools.partial(middle_kernel, quarters, landed, piece_rows),
        out_shape=jax.ShapeDtypeStruct((2, rows, cols), F32),
        in_specs=[vmem()] * (4 + len(arrays)),
        out_specs=vmem(),
        scratch_shapes=[pltpu.VMEM((len(quarters) * rows // 4, cols), F32)] * 2,
        compiler_params=params(),
        cost_estimate=cost(MIDDLE_COST),
        name="middle",
    )(*parts, *arrays)


def second_kernel(quarters, exchanged, grouped, landed, piece_rows, top_bit, *refs):
    sum_ref, pair_ref, own_ref, other_ref, group_ref = refs[4:9]
    landed_refs = refs[9 : 9 + len(landed)]
    out_ref = refs[-3]
    bit = (lax.axis_index("lo") >> top_bit) & 1
    c = pair_coefficients(pair_ref, 0, bit)
    pieces = {step: (ref[0], ref[1]) for step, ref in zip(landed, landed_refs, strict=True)}
    pieces.update(split_pieces(group_ref, grouped, piece_rows))
    others = split_pieces(other_ref, exchanged, piece_rows)
    for step, own in split_pieces(own_ref, exchanged, piece_rows).items():
        pieces[step] = combined(own, others[step], c)
    real, imag = partial_product(quarters, pieces, piece_rows, refs[:4], refs[-2:])
    out_ref[0] = sum_ref[0] + real
    out_ref[1] = sum_ref[1] + imag


def second(
    quarters, exchanged, grouped, landed, piece_rows, top_bit, parts, total, pair, own, other, arrays
):
    rows = parts[0].shape[0]
    cols = own.shape[2]
    return pl.pallas_call(
        functools.partial(
            second_kernel, quarters, exchanged, grouped, landed, piece_rows, top_bit
        ),
        out_shape=jax.ShapeDtypeStruct((2, rows, cols), F32),
        in_specs=[vmem()] * 5 + [smem()] + [vmem()] * (2 + len(arrays)),
        out_specs=vmem(),
        scratch_shapes=[pltpu.VMEM((len(quarters) * rows // 4, cols), F32)] * 2,
        compiler_params=params(),
        cost_estimate=cost(),
        name="second",
    )(*parts, total, pair, own, other, *arrays)


def last_kernel(own_ref, other_ref, coefficients_ref, out_ref):
    c = [coefficients_ref[i : i + 1, :] for i in range(4)]
    out_ref[0, 0], out_ref[1, 0] = combined(own_ref, other_ref, c)


def last(own, other, coefficients):
    _, rows, cols = own.shape
    step = rows // 4
    block = pl.BlockSpec((2, step, cols), lambda i: (0, i, 0))
    return pl.pallas_call(
        last_kernel,
        grid=(rows // step,),
        out_shape=jax.ShapeDtypeStruct((2, 1, rows, cols), F32),
        in_specs=[block, block, pl.BlockSpec((8, cols), lambda i: (0, 0))],
        out_specs=pl.BlockSpec((2, 1, step, cols), lambda i: (0, 0, i, 0)),
        compiler_params=params(),
        cost_estimate=cost(),
        name="last",
    )(own, other, coefficients)


def swap(value, axis, mask):
    return lax.ppermute(value, axis, [(i, i ^ mask) for i in range(lax.axis_size(axis))])


def after(value, earlier):
    return lax.optimization_barrier((value, earlier))[0]


def shards(amplitudes, gates, pair, angles, phases, bits, coupled, layout):
    rows = amplitudes.shape[2]
    cols = amplitudes.shape[3]
    col_bits = cols.bit_length() - 1
    count = lax.axis_size("hi")
    piece_rows = rows // count
    top_bit = lax.axis_size("lo").bit_length() - 2
    quarter = count // 4
    angles = angles.T
    beside = tuple(range(1, quarter))
    near = tuple(range(quarter, 2 * quarter))
    far = tuple(range(2 * quarter, 3 * quarter))
    early = tuple(range(3 * quarter, count))
    late = beside + far
    cross = functools.partial(swap, axis="lo", mask=1 << top_bit)

    made = first(
        (early, (0,) + near) + tuple((d,) for d in late),
        piece_rows,
        col_bits,
        amplitudes,
        gates,
        phases,
        angles,
        bits,
        coupled,
        layout,
    )
    early_part, near_part, *late_parts = made
    early_other = cross(early_part)
    late_parts = [swap(part, "hi", d) for part, d in zip(late_parts, late, strict=True)]
    near_other = cross(near_part)
    early_parts = combine(top_bit, len(early), early_part, early_other, pair)
    *parts, coefficients = ready(
        col_bits, after(gates, early_parts[0]), phases, angles, bits, coupled, pair
    )
    early_parts = [swap(part, "hi", d) for part, d in zip(early_parts, early, strict=True)]
    for part in late_parts[: len(beside)]:
        near_other = after(near_other, part)
    own_part, *near_parts = combine(
        top_bit, 1 + len(near), near_part, after(near_other, coefficients), pair
    )
    late_part = joined([after(part, own_part) for part in late_parts], LATE_COST)
    late_other = cross(late_part)
    near_parts = [swap(part, "hi", d) for part, d in zip(near_parts, near, strict=True)]
    half = len(early) // 2
    half_part = joined(early_parts[:half], HALF_COST)
    total = middle((1,), near, piece_rows, parts, [after(part, half_part) for part in near_parts])
    gated = second(
        (0, 2, 3),
        late,
        early[:half],
        (0,) + early[half:],
        piece_rows,
        top_bit,
        parts,
        total,
        pair,
        late_part,
        after(late_other, total),
        [half_part, own_part] + early_parts[half:],
    )
    return last(gated, swap(gated, "lo", 1), coefficients)


def solution(mesh):
    placed = (
        P(None, ("hi", "lo"), None, None),
        P(),
        P(),
        P(None, ("hi", "lo")),
        P(),
        P(),
        P(),
        P(),
    )
    return jax.shard_map(
        shards,
        mesh=mesh,
        in_specs=placed,
        out_specs=P(None, ("hi", "lo"), None, None),
        check_vma=False,
    )
```

```python
import functools

import jax
import jax.numpy as jnp
from jax import lax
from jax.experimental import pallas as pl
from jax.experimental.pallas import tpu as pltpu
from jax.sharding import PartitionSpec as P

F32 = jnp.float32
BF16 = jnp.bfloat16
VMEM_BYTES = 32 * 1024 * 1024
MIDDLE_COST = 3000000000
HALF_COST = 1000
READY_COST = 1500001000
LATE_COST = 1000


def sincos(x):
    turns = jnp.floor(x * 0.6366197723675814 + 0.5)
    r = x - turns * 1.5703125
    r = r - turns * 4.837512969970703125e-4
    r = r - turns * 7.54978995489188216e-8
    z = r * r
    sine = r + r * z * ((-1.9515295891e-4 * z + 8.3321608736e-3) * z - 1.6666654611e-1)
    cosine = 1.0 - 0.5 * z + z * z * (
        (2.443315711809948e-5 * z - 1.388731625493765e-3) * z + 4.166664568298827e-2
    )
    quarter = turns.astype(jnp.int32) & 3
    odd = (quarter & 1) == 1
    new_sine = jnp.where(odd, cosine, sine)
    new_cosine = jnp.where(odd, sine, cosine)
    new_sine = jnp.where((quarter & 2) == 2, -new_sine, new_sine)
    new_cosine = jnp.where(((quarter + 1) & 2) == 2, -new_cosine, new_cosine)
    return new_cosine, new_sine


def qubit_factors(layer, phases_ref, bits_ref, coupled_ref):
    qubits = phases_ref.shape[1]
    lane = lax.broadcasted_iota(jnp.int32, (1, qubits), 1)
    odd = jnp.zeros((1, qubits), jnp.int32)
    for f in range(bits_ref.shape[0]):
        odd = odd ^ jnp.where(lane == coupled_ref[layer, f], bits_ref[f], 0)
    sign = 1.0 - 2.0 * odd.astype(F32)
    cosine, sine = sincos(phases_ref[layer : layer + 1, :])
    return cosine * sign, sine * sign


def turn(real, imag, cosine, sine):
    return real * cosine - imag * sine, real * sine + imag * cosine


def row_phases(cosine, sine, first, row_bits, base_real, base_imag):
    sub = lax.broadcasted_iota(jnp.int32, (8, 128), 0)
    real = jnp.broadcast_to(base_real, (8, 128))
    imag = jnp.broadcast_to(base_imag, (8, 128))
    for k in range(row_bits):
        c = cosine[:, first + k : first + k + 1]
        s = sine[:, first + k : first + k + 1]
        if k < 3:
            chosen = ((sub >> k) & 1) == 1
            real, imag = turn(real, imag, jnp.where(chosen, c, 1.0), jnp.where(chosen, s, 0.0))
        else:
            up_real, up_imag = turn(real, imag, c, s)
            real = jnp.concatenate([real, up_real], axis=0)
            imag = jnp.concatenate([imag, up_imag], axis=0)
    return real, imag


def col_phases(cosine, sine, col_bits, cols):
    lane = lax.broadcasted_iota(jnp.int32, (1, cols), 1)
    real = jnp.ones((1, cols), F32)
    imag = jnp.zeros((1, cols), F32)
    for k in range(col_bits):
        chosen = ((lane >> k) & 1) == 1
        c = cosine[:, k : k + 1]
        s = sine[:, k : k + 1]
        real, imag = turn(real, imag, jnp.where(chosen, c, 1.0), jnp.where(chosen, s, 0.0))
    return real, imag


def split(x):
    high = x.astype(BF16)
    low = (x - high.astype(F32)).astype(BF16)
    return high, low


def dot(a, b):
    return jnp.dot(a, b, preferred_element_type=F32)


def signed_block(r, i):
    return jnp.concatenate(
        [jnp.concatenate([r, i], axis=1), jnp.concatenate([-i, r], axis=1)], axis=0
    )


def turned_rows(real, imag, phase_real, phase_imag):
    reps = real.shape[1] // phase_real.shape[1]
    phase_real = jnp.concatenate([phase_real] * reps, axis=1)
    phase_imag = jnp.concatenate([phase_imag] * reps, axis=1)
    real, imag = turn(real, imag, phase_real, phase_imag)
    real_high, real_low = split(real)
    imag_high, imag_low = split(imag)
    return signed_block(real_high, imag_high), signed_block(real_low, imag_low)


def product(left_high, left_low, right_high, right_low):
    return dot(left_high, right_high) + dot(left_high, right_low) + dot(left_low, right_high)


def hbm(array):
    return pltpu.with_memory_space_constraint(array, pltpu.HBM)


def any_space():
    return pl.BlockSpec(memory_space=pl.ANY)


def smem():
    return pl.BlockSpec(memory_space=pltpu.SMEM)


def vmem():
    return pl.BlockSpec(memory_space=pltpu.VMEM)


def cost(flops=1000):
    return pl.CostEstimate(flops=flops, bytes_accessed=1000, transcendentals=0)


def params():
    return pltpu.CompilerParams(vmem_limit_bytes=VMEM_BYTES)


def chosen_rows(steps, piece_rows, rows, layout_ref):
    me = lax.axis_index("hi")
    row_bits = rows.bit_length() - 1
    sub = lax.broadcasted_iota(jnp.int32, (8, 128), 0)
    inner = jnp.zeros((8, 128), jnp.int32)
    inner_bits = piece_rows.bit_length() - 1
    for k in range(inner_bits):
        place = jnp.left_shift(jnp.int32(1), layout_ref[k])
        if k < 3:
            inner = inner + ((sub >> k) & 1) * place
        else:
            inner = jnp.concatenate([inner, inner + place], axis=0)
    places = []
    for step in steps:
        block = me ^ step
        base = jnp.int32(0)
        for k in range(inner_bits, row_bits):
            base = base + jnp.left_shift((block >> (k - inner_bits)) & 1, layout_ref[k])
        places.append(inner + base)
    places = jnp.concatenate(places, axis=0)
    lane = lax.broadcasted_iota(jnp.int32, places.shape, 1)
    return jnp.concatenate(
        [
            jnp.where(places == lane + start, 1.0, 0.0).astype(BF16)
            for start in range(0, rows, 128)
        ],
        axis=1,
    )


def gate_pieces(groups, piece_rows, layout_ref, left_high, left_low, right_high, right_low, out_refs):
    rows = left_high.shape[0]
    cols = right_high.shape[1] // 2
    gated = product(left_high, left_low, right_high, right_low)
    chosen = chosen_rows([d for group in groups for d in group], piece_rows, rows, layout_ref)
    gated_high, gated_low = split(gated)
    out = dot(chosen, gated_high) + dot(chosen, gated_low)
    start = 0
    for group, out_ref in zip(groups, out_refs, strict=True):
        size = len(group) * piece_rows
        out_ref[0] = out[start : start + size, :cols]
        out_ref[1] = out[start : start + size, cols:]
        start += size


def first_kernel(
    groups,
    piece_rows,
    col_bits,
    amplitudes_hbm,
    gates_hbm,
    phases_hbm,
    angles_hbm,
    bits_hbm,
    coupled_hbm,
    layout_hbm,
    *refs,
):
    (
        *out_refs,
        amplitudes_ref,
        gates_ref,
        phases_ref,
        angles_ref,
        bits_ref,
        coupled_ref,
        layout_ref,
        sems,
    ) = refs
    copies = [
        pltpu.make_async_copy(source, target, sems.at[i])
        for i, (source, target) in enumerate(
            (
                (phases_hbm, phases_ref),
                (angles_hbm, angles_ref),
                (bits_hbm, bits_ref),
                (coupled_hbm, coupled_ref),
                (layout_hbm, layout_ref),
                (gates_hbm.at[0, 0], gates_ref.at[0]),
                (gates_hbm.at[0, 1], gates_ref.at[1]),
                (amplitudes_hbm, amplitudes_ref),
            )
        )
    ]
    for copy in copies:
        copy.start()
    for copy in copies[:5]:
        copy.wait()
    rows = amplitudes_ref.shape[2]
    row_bits = rows.bit_length() - 1
    cosine, sine = qubit_factors(0, phases_ref, bits_ref, coupled_ref)
    base_real, base_imag = sincos(angles_ref[0:1, 0:1])
    phase_real, phase_imag = row_phases(cosine, sine, col_bits, row_bits, base_real, base_imag)
    high, low = [], []
    for i in range(2):
        copies[5 + i].wait()
        for parts, part in zip((high, low), split(gates_ref[i]), strict=True):
            parts.append(part)
    copies[7].wait()
    right_high, right_low = turned_rows(
        amplitudes_ref[0, 0], amplitudes_ref[1, 0], phase_real, phase_imag
    )
    gate_pieces(
        groups,
        piece_rows,
        layout_ref,
        jnp.concatenate(high, axis=1),
        jnp.concatenate(low, axis=1),
        right_high,
        right_low,
        out_refs,
    )


def first(groups, piece_rows, col_bits, amplitudes, gates, phases, angles, bits, coupled, layout):
    rows, cols = amplitudes.shape[2:]
    shapes = [jax.ShapeDtypeStruct((2, len(group) * piece_rows, cols), F32) for group in groups]
    sources = (amplitudes, gates, phases, angles, bits, coupled, layout)
    return pl.pallas_call(
        functools.partial(first_kernel, groups, piece_rows, col_bits),
        out_shape=shapes,
        in_specs=[any_space()] * len(sources),
        out_specs=[vmem()] * len(shapes),
        scratch_shapes=[
            pltpu.VMEM(amplitudes.shape, F32),
            pltpu.VMEM(gates.shape[1:], F32),
            pltpu.VMEM(phases.shape, F32),
            pltpu.VMEM(angles.shape, F32),
            pltpu.SMEM(bits.shape, jnp.int32),
            pltpu.SMEM(coupled.shape, jnp.int32),
            pltpu.SMEM(layout.shape, jnp.int32),
            pltpu.SemaphoreType.DMA((8,)),
        ],
        compiler_params=params(),
        cost_estimate=cost(),
        name="first",
    )(*[hbm(source) for source in sources])


def own_order(tile, piece_rows, me):
    lane = lax.broadcasted_iota(jnp.int32, tile.shape, 1)
    width = tile.shape[1]
    size = piece_rows
    bit = 0
    while size < width:
        upper = (lane & size) != 0
        swapped = jnp.where(
            upper, pltpu.roll(tile, size, 1), pltpu.roll(tile, width - size, 1)
        )
        tile = jnp.where(((me >> bit) & 1) == 1, swapped, tile)
        size *= 2
        bit += 1
    return tile


def ready_kernel(
    sets, piece_rows, col_bits, gates_hbm, phases_ref, angles_ref, bits_ref, coupled_ref, pair_ref, *refs
):
    *out_refs, coefficients_ref, gates_ref, phase_real_ref, phase_imag_ref, sem = refs
    copy = pltpu.make_async_copy(gates_hbm.at[1], gates_ref, sem)
    copy.start()
    me = lax.axis_index("hi")
    rows = gates_ref.shape[1]
    cols = coefficients_ref.shape[1]
    row_bits = rows.bit_length() - 1
    bit = lax.axis_index("lo") & 1
    before = qubit_factors(0, phases_ref, bits_ref, coupled_ref)
    after = qubit_factors(1, phases_ref, bits_ref, coupled_ref)
    base_real, base_imag = sincos(angles_ref[0:1, 1:2])
    phase_real_ref[...], phase_imag_ref[...] = row_phases(
        *after, col_bits, row_bits, base_real, base_imag
    )
    phase_real, phase_imag = turn(
        *col_phases(*before, col_bits, cols), *col_phases(*after, col_bits, cols)
    )
    c = pair_coefficients(pair_ref, 1, bit)
    c = turn(phase_real, phase_imag, c[0], c[1]) + turn(phase_real, phase_imag, c[2], c[3])
    for i in range(4):
        coefficients_ref[i : i + 1, :] = c[i]
    coefficients_ref[4:8, :] = jnp.zeros((4, cols), F32)
    copy.wait()
    size = rows // 4
    quarter = size // piece_rows
    high, low = [], []
    for i in range(2):
        high_tiles, low_tiles = [], []
        for q in range(4):
            start = pl.multiple_of(((me // quarter) ^ q) * size, size)
            tile = own_order(gates_ref[i, :, pl.ds(start, size)], piece_rows, me)
            for tiles, part in zip((high_tiles, low_tiles), split(tile), strict=True):
                tiles.append(part)
        high.append(jnp.concatenate(high_tiles, axis=1))
        low.append(jnp.concatenate(low_tiles, axis=1))
    for k, steps in enumerate(sets):
        for part, out_ref in zip((high, low), out_refs[4 * k : 4 * k + 2], strict=True):
            out_ref[...] = jnp.concatenate(
                [
                    part[i][:, d * piece_rows : (d + 1) * piece_rows]
                    for i in range(2)
                    for d in steps
                ],
                axis=1,
            )
        for j, d in enumerate(steps):
            start = pl.multiple_of((me ^ d) * piece_rows, piece_rows)
            target = slice(j * piece_rows, (j + 1) * piece_rows)
            out_refs[4 * k + 2][target, :] = phase_real_ref[pl.ds(start, piece_rows), :]
            out_refs[4 * k + 3][target, :] = phase_imag_ref[pl.ds(start, piece_rows), :]


def ready(sets, piece_rows, col_bits, gates, phases, angles, bits, coupled, pair):
    rows = gates.shape[2]
    cols = 1 << col_bits
    shapes = []
    for steps in sets:
        depth = len(steps) * piece_rows
        shapes += [jax.ShapeDtypeStruct((rows, 2 * depth), BF16)] * 2
        shapes += [jax.ShapeDtypeStruct((depth, 128), F32)] * 2
    shapes.append(jax.ShapeDtypeStruct((8, cols), F32))
    return pl.pallas_call(
        functools.partial(ready_kernel, sets, piece_rows, col_bits),
        out_shape=shapes,
        in_specs=[any_space(), vmem(), vmem(), smem(), smem(), smem()],
        out_specs=[vmem()] * len(shapes),
        scratch_shapes=[
            pltpu.VMEM(gates.shape[1:], F32),
            pltpu.VMEM((rows, 128), F32),
            pltpu.VMEM((rows, 128), F32),
            pltpu.SemaphoreType.DMA,
        ],
        compiler_params=params(),
        cost_estimate=cost(READY_COST),
        name="ready",
    )(hbm(gates), phases, angles, bits, coupled, pair)


def pair_coefficients(pair_ref, layer, bit):
    own = bit
    other = 1 - bit
    return (
        pair_ref[layer, 0, own, own],
        pair_ref[layer, 1, own, own],
        pair_ref[layer, 0, own, other],
        pair_ref[layer, 1, own, other],
    )


def combined(own, other, c):
    own_real, own_imag = turn(own[0], own[1], c[0], c[1])
    other_real, other_imag = turn(other[0], other[1], c[2], c[3])
    return own_real + other_real, own_imag + other_imag


def combine_kernel(top_bit, own_ref, other_ref, pair_ref, *out_refs):
    bit = (lax.axis_index("lo") >> top_bit) & 1
    c = pair_coefficients(pair_ref, 0, bit)
    size = out_refs[0].shape[1]
    for i, out_ref in enumerate(out_refs):
        rows = slice(i * size, (i + 1) * size)
        out_ref[0], out_ref[1] = combined(
            (own_ref[0, rows], own_ref[1, rows]), (other_ref[0, rows], other_ref[1, rows]), c
        )


def combine(top_bit, count, own, other, pair_gates):
    shape = (2, own.shape[1] // count, own.shape[2])
    return pl.pallas_call(
        functools.partial(combine_kernel, top_bit),
        out_shape=[jax.ShapeDtypeStruct(shape, F32)] * count,
        in_specs=[vmem(), vmem(), smem()],
        out_specs=[vmem()] * count,
        compiler_params=params(),
        cost_estimate=cost(),
        name="combine",
    )(own, other, pair_gates)


def late_kernel(*refs):
    *part_refs, out_ref = refs
    size = part_refs[0].shape[1]
    for i, part_ref in enumerate(part_refs):
        out_ref[:, i * size : (i + 1) * size, :] = part_ref[...]


def joined(arrays, flops):
    _, size, cols = arrays[0].shape
    return pl.pallas_call(
        late_kernel,
        out_shape=jax.ShapeDtypeStruct((2, size * len(arrays), cols), F32),
        in_specs=[vmem()] * len(arrays),
        out_specs=vmem(),
        compiler_params=params(),
        cost_estimate=cost(flops),
        name="joined",
    )(*arrays)


def turned_pieces_kernel(phase_real_ref, phase_imag_ref, *refs):
    *piece_refs, out_ref = refs
    reps = out_ref.shape[2] // phase_real_ref.shape[1]
    start = 0
    for ref in piece_refs:
        part = slice(start, start + ref.shape[1])
        cosine = jnp.concatenate([phase_real_ref[part, :]] * reps, axis=1)
        sine = jnp.concatenate([phase_imag_ref[part, :]] * reps, axis=1)
        out_ref[0, part], out_ref[1, part] = turn(ref[0], ref[1], cosine, sine)
        start += ref.shape[1]


def turned_pieces(phase_parts, arrays):
    shape = (2, sum(a.shape[1] for a in arrays), arrays[0].shape[2])
    return pl.pallas_call(
        turned_pieces_kernel,
        out_shape=jax.ShapeDtypeStruct(shape, F32),
        in_specs=[vmem()] * (2 + len(arrays)),
        out_specs=vmem(),
        compiler_params=params(),
        cost_estimate=cost(MIDDLE_COST),
        name="turned_pieces",
    )(*phase_parts, *arrays)


def mixed_parts(coefficients_ref, own_ref, other_ref):
    c = [coefficients_ref[i : i + 1, :] for i in range(4)]
    real, imag = combined(own_ref, other_ref, c)
    real_high, real_low = split(real)
    imag_high, imag_low = split(imag)
    return signed_block(real_high, imag_high), signed_block(real_low, imag_low)


def middle_kernel(high_ref, low_ref, coefficients_ref, own_ref, other_ref, out_ref):
    cols = out_ref.shape[2]
    right_high, right_low = mixed_parts(coefficients_ref, own_ref, other_ref)
    out = product(high_ref[...], low_ref[...], right_high, right_low)
    out_ref[0] = out[:, :cols]
    out_ref[1] = out[:, cols:]


def middle(parts, coefficients, own, other):
    return pl.pallas_call(
        middle_kernel,
        out_shape=jax.ShapeDtypeStruct((2, parts[0].shape[0], own.shape[2]), F32),
        in_specs=[vmem()] * 5,
        out_specs=vmem(),
        compiler_params=params(),
        cost_estimate=cost(),
        name="middle",
    )(*parts, coefficients, own, other)


def turned_kernel(
    top_bit, phase_real_ref, phase_imag_ref, pair_ref, own_ref, other_ref, last_ref, out_ref
):
    bit = (lax.axis_index("lo") >> top_bit) & 1
    size = own_ref.shape[1]
    parts = (
        (slice(0, size), combined(own_ref, other_ref, pair_coefficients(pair_ref, 0, bit))),
        (slice(size, out_ref.shape[1]), (last_ref[0], last_ref[1])),
    )
    reps = out_ref.shape[2] // phase_real_ref.shape[1]
    for part, (real, imag) in parts:
        cosine = jnp.concatenate([phase_real_ref[part, :]] * reps, axis=1)
        sine = jnp.concatenate([phase_imag_ref[part, :]] * reps, axis=1)
        out_ref[0, part], out_ref[1, part] = turn(real, imag, cosine, sine)


def turned(top_bit, phase_parts, pair, own, other, last):
    shape = (2, own.shape[1] + last.shape[1], own.shape[2])
    return pl.pallas_call(
        functools.partial(turned_kernel, top_bit),
        out_shape=jax.ShapeDtypeStruct(shape, F32),
        in_specs=[vmem(), vmem(), smem(), vmem(), vmem(), vmem()],
        out_specs=vmem(),
        compiler_params=params(),
        cost_estimate=cost(),
        name="turned",
    )(*phase_parts, pair, own, other, last)


def last_kernel(
    high_ref, low_ref, coefficients_ref, own_ref, other_ref, sum_ref, out_hbm, out_ref, sems
):
    cols = own_ref.shape[2]
    right_high, right_low = mixed_parts(coefficients_ref, own_ref, other_ref)
    count = sems.shape[0]
    step = out_ref.shape[2] // count
    copies = []
    for i in range(count):
        part = pl.ds(i * step, step)
        out = product(high_ref[part, :], low_ref[part, :], right_high, right_low)
        out_ref[0, 0, part] = sum_ref[0, part] + out[:, :cols]
        out_ref[1, 0, part] = sum_ref[1, part] + out[:, cols:]
        copies.append(
            pltpu.make_async_copy(
                out_ref.at[:, :, part], out_hbm.at[:, :, part], sems.at[i]
            )
        )
        copies[-1].start()
    for copy in copies:
        copy.wait()


def last(parts, coefficients, own, other, total):
    _, rows, cols = total.shape
    shape = (2, 1, rows, cols)
    return pl.pallas_call(
        last_kernel,
        out_shape=jax.ShapeDtypeStruct(shape, F32),
        in_specs=[vmem()] * 6,
        out_specs=any_space(),
        scratch_shapes=[pltpu.VMEM(shape, F32), pltpu.SemaphoreType.DMA((2,))],
        compiler_params=params(),
        cost_estimate=cost(),
        name="last",
    )(*parts, coefficients, own, other, total)


def swap(value, axis, mask):
    return lax.ppermute(value, axis, [(i, i ^ mask) for i in range(lax.axis_size(axis))])


def after(value, earlier):
    return lax.optimization_barrier((value, earlier))[0]


def shards(amplitudes, gates, pair, angles, phases, bits, coupled, layout):
    rows = amplitudes.shape[2]
    cols = amplitudes.shape[3]
    col_bits = cols.bit_length() - 1
    count = lax.axis_size("hi")
    piece_rows = rows // count
    top_bit = lax.axis_size("lo").bit_length() - 2
    quarter = count // 4
    angles = angles.T
    beside = tuple(range(1, quarter))
    near = tuple(range(quarter, 2 * quarter))
    far = tuple(range(2 * quarter, 3 * quarter))
    early = tuple(range(3 * quarter, count))
    late = beside + far
    cross = functools.partial(swap, axis="lo", mask=1 << top_bit)

    made = first(
        (early, (0,) + near) + tuple((d,) for d in late),
        piece_rows,
        col_bits,
        amplitudes,
        gates,
        phases,
        angles,
        bits,
        coupled,
        layout,
    )
    early_part, near_part, *late_parts = made
    early_other = cross(early_part)
    late_parts = [swap(part, "hi", d) for part, d in zip(late_parts, late, strict=True)]
    near_other = cross(near_part)
    early_parts = combine(top_bit, len(early), early_part, early_other, pair)
    sets = ((0,) + near + early[:-1], late + early[-1:])
    *parts, coefficients = ready(
        sets, piece_rows, col_bits, after(gates, early_parts[0]), phases, angles, bits, coupled, pair
    )
    early_parts = [swap(part, "hi", d) for part, d in zip(early_parts, early, strict=True)]
    own_part, *near_parts = combine(
        top_bit, 1 + len(near), near_part, after(near_other, coefficients), pair
    )
    late_part = joined([after(part, own_part) for part in late_parts], LATE_COST)
    late_other = cross(late_part)
    near_parts = [swap(part, "hi", d) for part, d in zip(near_parts, near, strict=True)]
    half_part = joined(early_parts[:-1], HALF_COST)
    near_turned = turned_pieces(
        parts[2:4], [own_part] + [after(part, half_part) for part in near_parts] + [half_part]
    )
    near_turned_other = swap(near_turned, "lo", 1)
    late_turned = turned(
        top_bit, parts[6:], pair, late_part, after(late_other, near_turned), early_parts[-1]
    )
    late_turned_other = swap(late_turned, "lo", 1)
    total = middle(parts[:2], coefficients, near_turned, near_turned_other)
    return last(parts[4:6], coefficients, late_turned, late_turned_other, total)


def solution(mesh):
    placed = (
        P(None, ("hi", "lo"), None, None),
        P(),
        P(),
        P(None, ("hi", "lo")),
        P(),
        P(),
        P(),
        P(),
    )
    return jax.shard_map(
        shards,
        mesh=mesh,
        in_specs=placed,
        out_specs=P(None, ("hi", "lo"), None, None),
        check_vma=False,
    )
```

```python
import functools

import jax
import jax.numpy as jnp
from jax import lax
from jax.experimental import pallas as pl
from jax.experimental.pallas import tpu as pltpu
from jax.sharding import PartitionSpec as P

F32 = jnp.float32
BF16 = jnp.bfloat16
VMEM_BYTES = 32 * 1024 * 1024
MIDDLE_COST = 3000000000
HALF_COST = 1000
CHUNKS = 2
LAST_CHUNKS = 4
COMBINE_COST = 1500001000
LATE_COST = 1000


def sincos(x):
    turns = jnp.floor(x * 0.6366197723675814 + 0.5)
    r = x - turns * 1.5703125
    r = r - turns * 4.837512969970703125e-4
    r = r - turns * 7.54978995489188216e-8
    z = r * r
    sine = r + r * z * ((-1.9515295891e-4 * z + 8.3321608736e-3) * z - 1.6666654611e-1)
    cosine = 1.0 - 0.5 * z + z * z * (
        (2.443315711809948e-5 * z - 1.388731625493765e-3) * z + 4.166664568298827e-2
    )
    quarter = turns.astype(jnp.int32) & 3
    odd = (quarter & 1) == 1
    new_sine = jnp.where(odd, cosine, sine)
    new_cosine = jnp.where(odd, sine, cosine)
    new_sine = jnp.where((quarter & 2) == 2, -new_sine, new_sine)
    new_cosine = jnp.where(((quarter + 1) & 2) == 2, -new_cosine, new_cosine)
    return new_cosine, new_sine


def qubit_factors(layer, phases_ref, bits_ref, coupled_ref):
    qubits = phases_ref.shape[1]
    lane = lax.broadcasted_iota(jnp.int32, (1, qubits), 1)
    odd = jnp.zeros((1, qubits), jnp.int32)
    for f in range(bits_ref.shape[0]):
        odd = odd ^ jnp.where(lane == coupled_ref[layer, f], bits_ref[f], 0)
    sign = 1.0 - 2.0 * odd.astype(F32)
    cosine, sine = sincos(phases_ref[layer : layer + 1, :])
    return cosine * sign, sine * sign


def turn(real, imag, cosine, sine):
    return real * cosine - imag * sine, real * sine + imag * cosine


def row_phases(cosine, sine, first, row_bits, base_real, base_imag):
    sub = lax.broadcasted_iota(jnp.int32, (8, 128), 0)
    real = jnp.broadcast_to(base_real, (8, 128))
    imag = jnp.broadcast_to(base_imag, (8, 128))
    for k in range(row_bits):
        c = cosine[:, first + k : first + k + 1]
        s = sine[:, first + k : first + k + 1]
        if k < 3:
            chosen = ((sub >> k) & 1) == 1
            real, imag = turn(real, imag, jnp.where(chosen, c, 1.0), jnp.where(chosen, s, 0.0))
        else:
            up_real, up_imag = turn(real, imag, c, s)
            real = jnp.concatenate([real, up_real], axis=0)
            imag = jnp.concatenate([imag, up_imag], axis=0)
    return real, imag


def col_phases(cosine, sine, col_bits, cols):
    lane = lax.broadcasted_iota(jnp.int32, (1, cols), 1)
    real = jnp.ones((1, cols), F32)
    imag = jnp.zeros((1, cols), F32)
    for k in range(col_bits):
        chosen = ((lane >> k) & 1) == 1
        c = cosine[:, k : k + 1]
        s = sine[:, k : k + 1]
        real, imag = turn(real, imag, jnp.where(chosen, c, 1.0), jnp.where(chosen, s, 0.0))
    return real, imag


def split(x):
    high = x.astype(BF16)
    low = (x - high.astype(F32)).astype(BF16)
    return high, low


def dot(a, b):
    return jnp.dot(a, b, preferred_element_type=F32)


def signed_block(r, i):
    return jnp.concatenate(
        [jnp.concatenate([r, i], axis=1), jnp.concatenate([-i, r], axis=1)], axis=0
    )


def turned_rows(real, imag, phase_real, phase_imag):
    reps = real.shape[1] // phase_real.shape[1]
    phase_real = jnp.concatenate([phase_real] * reps, axis=1)
    phase_imag = jnp.concatenate([phase_imag] * reps, axis=1)
    real, imag = turn(real, imag, phase_real, phase_imag)
    real_high, real_low = split(real)
    imag_high, imag_low = split(imag)
    return signed_block(real_high, imag_high), signed_block(real_low, imag_low)


def product(left_high, left_low, right_high, right_low):
    return dot(left_high, right_high) + dot(left_high, right_low) + dot(left_low, right_high)


def hbm(array):
    return pltpu.with_memory_space_constraint(array, pltpu.HBM)


def any_space():
    return pl.BlockSpec(memory_space=pl.ANY)


def smem():
    return pl.BlockSpec(memory_space=pltpu.SMEM)


def vmem():
    return pl.BlockSpec(memory_space=pltpu.VMEM)


def cost(flops=1000):
    return pl.CostEstimate(flops=flops, bytes_accessed=1000, transcendentals=0)


def params():
    return pltpu.CompilerParams(vmem_limit_bytes=VMEM_BYTES)


def chosen_rows(steps, piece_rows, rows, layout_ref):
    me = lax.axis_index("hi")
    row_bits = rows.bit_length() - 1
    sub = lax.broadcasted_iota(jnp.int32, (8, 128), 0)
    inner = jnp.zeros((8, 128), jnp.int32)
    inner_bits = piece_rows.bit_length() - 1
    for k in range(inner_bits):
        place = jnp.left_shift(jnp.int32(1), layout_ref[k])
        if k < 3:
            inner = inner + ((sub >> k) & 1) * place
        else:
            inner = jnp.concatenate([inner, inner + place], axis=0)
    places = []
    for step in steps:
        block = me ^ step
        base = jnp.int32(0)
        for k in range(inner_bits, row_bits):
            base = base + jnp.left_shift((block >> (k - inner_bits)) & 1, layout_ref[k])
        places.append(inner + base)
    places = jnp.concatenate(places, axis=0)
    lane = lax.broadcasted_iota(jnp.int32, places.shape, 1)
    return jnp.concatenate(
        [
            jnp.where(places == lane + start, 1.0, 0.0).astype(BF16)
            for start in range(0, rows, 128)
        ],
        axis=1,
    )


def first_kernel(
    groups,
    piece_rows,
    col_bits,
    top_bit,
    amplitudes_hbm,
    gates_hbm,
    phases_hbm,
    angles_hbm,
    bits_hbm,
    coupled_hbm,
    layout_hbm,
    pair_hbm,
    *refs,
):
    (
        pairs_ref,
        *out_refs,
        amplitudes_ref,
        gates_ref,
        phases_ref,
        angles_ref,
        bits_ref,
        coupled_ref,
        layout_ref,
        pair_ref,
        small_sems,
        chunk_sems,
    ) = refs
    rows, cols = amplitudes_ref.shape[2:]
    row_bits = rows.bit_length() - 1
    small = [
        pltpu.make_async_copy(source, target, small_sems.at[i])
        for i, (source, target) in enumerate(
            (
                (phases_hbm, phases_ref),
                (angles_hbm, angles_ref),
                (bits_hbm, bits_ref),
                (coupled_hbm, coupled_ref),
                (layout_hbm, layout_ref),
                (pair_hbm, pair_ref),
            )
        )
    ]
    count = chunk_sems.shape[0]
    step = rows // count
    chunks = []
    for k in range(count):
        part = pl.ds(k * step, step)
        chunks.append(
            [
                pltpu.make_async_copy(
                    gates_hbm.at[0, 0, :, part], gates_ref.at[0, :, part], chunk_sems.at[k, 0]
                ),
                pltpu.make_async_copy(
                    gates_hbm.at[0, 1, :, part], gates_ref.at[1, :, part], chunk_sems.at[k, 1]
                ),
                pltpu.make_async_copy(
                    amplitudes_hbm.at[:, :, part], amplitudes_ref.at[:, :, part], chunk_sems.at[k, 2]
                ),
            ]
        )
    for copy in small:
        copy.start()
    for chunk in chunks:
        for copy in chunk:
            copy.start()
    for copy in small:
        copy.wait()
    bit = (lax.axis_index("lo") >> top_bit) & 1
    c = pair_coefficients(pair_ref, 0, bit)
    for i in range(4):
        pairs_ref[i : i + 1, :] = jnp.full((1, cols), c[i], F32)
    pairs_ref[4:8, :] = jnp.zeros((4, cols), F32)
    cosine, sine = qubit_factors(0, phases_ref, bits_ref, coupled_ref)
    base_real, base_imag = sincos(angles_ref[0:1, 0:1])
    phase_real, phase_imag = row_phases(cosine, sine, col_bits, row_bits, base_real, base_imag)
    steps = [d for group in groups for d in group]
    chosen = chosen_rows(steps, piece_rows, rows, layout_ref)
    gated = None
    for k in range(count):
        for copy in chunks[k]:
            copy.wait()
        part = slice(k * step, (k + 1) * step)
        real_high, real_low = split(gates_ref[0, :, part])
        imag_high, imag_low = split(gates_ref[1, :, part])
        right_high, right_low = turned_rows(
            amplitudes_ref[0, 0, part], amplitudes_ref[1, 0, part], phase_real[part], phase_imag[part]
        )
        term = product(
            jnp.concatenate([real_high, imag_high], axis=1),
            jnp.concatenate([real_low, imag_low], axis=1),
            right_high,
            right_low,
        )
        gated = term if gated is None else gated + term
    gated_high, gated_low = split(gated)
    out = dot(chosen, gated_high) + dot(chosen, gated_low)
    start = 0
    for group, out_ref in zip(groups, out_refs, strict=True):
        size = len(group) * piece_rows
        out_ref[0] = out[start : start + size, :cols]
        out_ref[1] = out[start : start + size, cols:]
        start += size


def first(
    groups, piece_rows, col_bits, top_bit, amplitudes, gates, phases, angles, bits, coupled, layout, pair
):
    rows, cols = amplitudes.shape[2:]
    shapes = [jax.ShapeDtypeStruct((8, cols), F32)]
    shapes += [jax.ShapeDtypeStruct((2, len(group) * piece_rows, cols), F32) for group in groups]
    sources = (amplitudes, gates, phases, angles, bits, coupled, layout, pair)
    return pl.pallas_call(
        functools.partial(first_kernel, groups, piece_rows, col_bits, top_bit),
        out_shape=shapes,
        in_specs=[any_space()] * len(sources),
        out_specs=[vmem()] * len(shapes),
        scratch_shapes=[
            pltpu.VMEM(amplitudes.shape, F32),
            pltpu.VMEM(gates.shape[1:], F32),
            pltpu.VMEM(phases.shape, F32),
            pltpu.VMEM(angles.shape, F32),
            pltpu.SMEM(bits.shape, jnp.int32),
            pltpu.SMEM(coupled.shape, jnp.int32),
            pltpu.SMEM(layout.shape, jnp.int32),
            pltpu.SMEM(pair.shape, F32),
            pltpu.SemaphoreType.DMA((6,)),
            pltpu.SemaphoreType.DMA((CHUNKS, 3)),
        ],
        compiler_params=params(),
        cost_estimate=cost(),
        name="first",
    )(*[hbm(source) for source in sources])


def own_order(tile, piece_rows, me):
    lane = lax.broadcasted_iota(jnp.int32, tile.shape, 1)
    width = tile.shape[1]
    size = piece_rows
    bit = 0
    while size < width:
        upper = (lane & size) != 0
        swapped = jnp.where(
            upper, pltpu.roll(tile, size, 1), pltpu.roll(tile, width - size, 1)
        )
        tile = jnp.where(((me >> bit) & 1) == 1, swapped, tile)
        size *= 2
        bit += 1
    return tile


def phases_kernel(
    sets, piece_rows, col_bits, phases_ref, angles_ref, bits_ref, coupled_ref, pair_ref, *refs
):
    *out_refs, coefficients_ref, phase_real_ref, phase_imag_ref = refs
    me = lax.axis_index("hi")
    rows = phase_real_ref.shape[0]
    cols = coefficients_ref.shape[1]
    row_bits = rows.bit_length() - 1
    bit = lax.axis_index("lo") & 1
    before = qubit_factors(0, phases_ref, bits_ref, coupled_ref)
    after = qubit_factors(1, phases_ref, bits_ref, coupled_ref)
    base_real, base_imag = sincos(angles_ref[0:1, 1:2])
    phase_real_ref[...], phase_imag_ref[...] = row_phases(
        *after, col_bits, row_bits, base_real, base_imag
    )
    phase_real, phase_imag = turn(
        *col_phases(*before, col_bits, cols), *col_phases(*after, col_bits, cols)
    )
    c = pair_coefficients(pair_ref, 1, bit)
    c = turn(phase_real, phase_imag, c[0], c[1]) + turn(phase_real, phase_imag, c[2], c[3])
    for i in range(4):
        coefficients_ref[i : i + 1, :] = c[i]
    coefficients_ref[4:8, :] = jnp.zeros((4, cols), F32)
    for k, steps in enumerate(sets):
        for j, d in enumerate(steps):
            start = pl.multiple_of((me ^ d) * piece_rows, piece_rows)
            target = slice(j * piece_rows, (j + 1) * piece_rows)
            out_refs[2 * k][target, :] = phase_real_ref[pl.ds(start, piece_rows), :]
            out_refs[2 * k + 1][target, :] = phase_imag_ref[pl.ds(start, piece_rows), :]


def second_phases(sets, piece_rows, rows, col_bits, phases, angles, bits, coupled, pair):
    cols = 1 << col_bits
    shapes = []
    for steps in sets:
        shapes += [jax.ShapeDtypeStruct((len(steps) * piece_rows, 128), F32)] * 2
    shapes.append(jax.ShapeDtypeStruct((8, cols), F32))
    return pl.pallas_call(
        functools.partial(phases_kernel, sets, piece_rows, col_bits),
        out_shape=shapes,
        in_specs=[vmem(), vmem(), smem(), smem(), smem()],
        out_specs=[vmem()] * len(shapes),
        scratch_shapes=[pltpu.VMEM((rows, 128), F32)] * 2,
        compiler_params=params(),
        cost_estimate=cost(),
        name="second_phases",
    )(phases, angles, bits, coupled, pair)


def gates_kernel(sets, piece_rows, gates_hbm, *refs):
    *out_refs, gates_ref, sem = refs
    copy = pltpu.make_async_copy(gates_hbm.at[1], gates_ref, sem)
    copy.start()
    me = lax.axis_index("hi")
    size = gates_ref.shape[1] // 4
    quarter = size // piece_rows
    copy.wait()
    high, low = [], []
    for i in range(2):
        high_tiles, low_tiles = [], []
        for q in range(4):
            start = pl.multiple_of(((me // quarter) ^ q) * size, size)
            tile = own_order(gates_ref[i, :, pl.ds(start, size)], piece_rows, me)
            for tiles, part in zip((high_tiles, low_tiles), split(tile), strict=True):
                tiles.append(part)
        high.append(jnp.concatenate(high_tiles, axis=1))
        low.append(jnp.concatenate(low_tiles, axis=1))
    for k, steps in enumerate(sets):
        for part, out_ref in zip((high, low), out_refs[2 * k : 2 * k + 2], strict=True):
            out_ref[...] = jnp.concatenate(
                [
                    part[i][:, d * piece_rows : (d + 1) * piece_rows]
                    for i in range(2)
                    for d in steps
                ],
                axis=1,
            )


def second_gates(sets, piece_rows, gates):
    rows = gates.shape[2]
    shapes = []
    for steps in sets:
        shapes += [jax.ShapeDtypeStruct((rows, 2 * len(steps) * piece_rows), BF16)] * 2
    return pl.pallas_call(
        functools.partial(gates_kernel, sets, piece_rows),
        out_shape=shapes,
        in_specs=[any_space()],
        out_specs=[vmem()] * len(shapes),
        scratch_shapes=[pltpu.VMEM(gates.shape[1:], F32), pltpu.SemaphoreType.DMA],
        compiler_params=params(),
        cost_estimate=cost(),
        name="second_gates",
    )(hbm(gates))


def pair_coefficients(pair_ref, layer, bit):
    own = bit
    other = 1 - bit
    return (
        pair_ref[layer, 0, own, own],
        pair_ref[layer, 1, own, own],
        pair_ref[layer, 0, own, other],
        pair_ref[layer, 1, own, other],
    )


def combined(own, other, c):
    own_real, own_imag = turn(own[0], own[1], c[0], c[1])
    other_real, other_imag = turn(other[0], other[1], c[2], c[3])
    return own_real + other_real, own_imag + other_imag


def vector_coefficients(ref):
    return [ref[i : i + 1, :] for i in range(4)]


def combine_kernel(pairs_ref, own_ref, other_ref, *out_refs):
    c = vector_coefficients(pairs_ref)
    size = out_refs[0].shape[1]
    for i, out_ref in enumerate(out_refs):
        rows = slice(i * size, (i + 1) * size)
        out_ref[0], out_ref[1] = combined(
            (own_ref[0, rows], own_ref[1, rows]), (other_ref[0, rows], other_ref[1, rows]), c
        )


def combine(count, own, other, pairs, flops):
    shape = (2, own.shape[1] // count, own.shape[2])
    return pl.pallas_call(
        combine_kernel,
        out_shape=[jax.ShapeDtypeStruct(shape, F32)] * count,
        in_specs=[vmem()] * 3,
        out_specs=[vmem()] * count,
        compiler_params=params(),
        cost_estimate=cost(flops),
        name="combine",
    )(pairs, own, other)


def late_kernel(*refs):
    *part_refs, out_ref = refs
    size = part_refs[0].shape[1]
    for i, part_ref in enumerate(part_refs):
        out_ref[:, i * size : (i + 1) * size, :] = part_ref[...]


def joined(arrays, flops):
    _, size, cols = arrays[0].shape
    return pl.pallas_call(
        late_kernel,
        out_shape=jax.ShapeDtypeStruct((2, size * len(arrays), cols), F32),
        in_specs=[vmem()] * len(arrays),
        out_specs=vmem(),
        compiler_params=params(),
        cost_estimate=cost(flops),
        name="joined",
    )(*arrays)


def turned_pieces_kernel(phase_real_ref, phase_imag_ref, *refs):
    *piece_refs, out_ref = refs
    reps = out_ref.shape[2] // phase_real_ref.shape[1]
    start = 0
    for ref in piece_refs:
        part = slice(start, start + ref.shape[1])
        cosine = jnp.concatenate([phase_real_ref[part, :]] * reps, axis=1)
        sine = jnp.concatenate([phase_imag_ref[part, :]] * reps, axis=1)
        out_ref[0, part], out_ref[1, part] = turn(ref[0], ref[1], cosine, sine)
        start += ref.shape[1]


def turned_pieces(phase_parts, arrays):
    shape = (2, sum(a.shape[1] for a in arrays), arrays[0].shape[2])
    return pl.pallas_call(
        turned_pieces_kernel,
        out_shape=jax.ShapeDtypeStruct(shape, F32),
        in_specs=[vmem()] * (2 + len(arrays)),
        out_specs=vmem(),
        compiler_params=params(),
        cost_estimate=cost(MIDDLE_COST),
        name="turned_pieces",
    )(*phase_parts, *arrays)


def mixed_parts(coefficients_ref, own_ref, other_ref):
    c = vector_coefficients(coefficients_ref)
    real, imag = combined(own_ref, other_ref, c)
    real_high, real_low = split(real)
    imag_high, imag_low = split(imag)
    return signed_block(real_high, imag_high), signed_block(real_low, imag_low)


def middle_kernel(high_ref, low_ref, coefficients_ref, own_ref, other_ref, out_ref):
    cols = out_ref.shape[2]
    right_high, right_low = mixed_parts(coefficients_ref, own_ref, other_ref)
    out = product(high_ref[...], low_ref[...], right_high, right_low)
    out_ref[0] = out[:, :cols]
    out_ref[1] = out[:, cols:]


def middle(parts, coefficients, own, other):
    return pl.pallas_call(
        middle_kernel,
        out_shape=jax.ShapeDtypeStruct((2, parts[0].shape[0], own.shape[2]), F32),
        in_specs=[vmem()] * 5,
        out_specs=vmem(),
        compiler_params=params(),
        cost_estimate=cost(),
        name="middle",
    )(*parts, coefficients, own, other)


def turned_kernel(
    phase_real_ref, phase_imag_ref, pairs_ref, own_ref, other_ref, last_ref, out_ref
):
    size = own_ref.shape[1]
    parts = (
        (slice(0, size), combined(own_ref, other_ref, vector_coefficients(pairs_ref))),
        (slice(size, out_ref.shape[1]), (last_ref[0], last_ref[1])),
    )
    reps = out_ref.shape[2] // phase_real_ref.shape[1]
    for part, (real, imag) in parts:
        cosine = jnp.concatenate([phase_real_ref[part, :]] * reps, axis=1)
        sine = jnp.concatenate([phase_imag_ref[part, :]] * reps, axis=1)
        out_ref[0, part], out_ref[1, part] = turn(real, imag, cosine, sine)


def turned(phase_parts, pairs, own, other, last):
    shape = (2, own.shape[1] + last.shape[1], own.shape[2])
    return pl.pallas_call(
        turned_kernel,
        out_shape=jax.ShapeDtypeStruct(shape, F32),
        in_specs=[vmem()] * 6,
        out_specs=vmem(),
        compiler_params=params(),
        cost_estimate=cost(),
        name="turned",
    )(*phase_parts, pairs, own, other, last)


def last_kernel(
    high_ref, low_ref, coefficients_ref, own_ref, other_ref, sum_ref, out_hbm, out_ref, sems
):
    cols = own_ref.shape[2]
    right_high, right_low = mixed_parts(coefficients_ref, own_ref, other_ref)
    count = sems.shape[0]
    step = out_ref.shape[2] // count
    copies = []
    for i in range(count):
        part = pl.ds(i * step, step)
        out = product(high_ref[part, :], low_ref[part, :], right_high, right_low)
        out_ref[0, 0, part] = sum_ref[0, part] + out[:, :cols]
        out_ref[1, 0, part] = sum_ref[1, part] + out[:, cols:]
        copies.append(
            pltpu.make_async_copy(
                out_ref.at[:, :, part], out_hbm.at[:, :, part], sems.at[i]
            )
        )
        copies[-1].start()
    for copy in copies:
        copy.wait()


def last(parts, coefficients, own, other, total):
    _, rows, cols = total.shape
    shape = (2, 1, rows, cols)
    return pl.pallas_call(
        last_kernel,
        out_shape=jax.ShapeDtypeStruct(shape, F32),
        in_specs=[vmem()] * 6,
        out_specs=any_space(),
        scratch_shapes=[pltpu.VMEM(shape, F32), pltpu.SemaphoreType.DMA((LAST_CHUNKS,))],
        compiler_params=params(),
        cost_estimate=cost(),
        name="last",
    )(*parts, coefficients, own, other, total)


def swap(value, axis, mask):
    return lax.ppermute(value, axis, [(i, i ^ mask) for i in range(lax.axis_size(axis))])


def after(value, earlier):
    return lax.optimization_barrier((value, earlier))[0]


def shards(amplitudes, gates, pair, angles, phases, bits, coupled, layout):
    rows = amplitudes.shape[2]
    cols = amplitudes.shape[3]
    col_bits = cols.bit_length() - 1
    count = lax.axis_size("hi")
    piece_rows = rows // count
    top_bit = lax.axis_size("lo").bit_length() - 2
    quarter = count // 4
    angles = angles.T
    beside = tuple(range(1, quarter))
    near = tuple(range(quarter, 2 * quarter))
    far = tuple(range(2 * quarter, 3 * quarter))
    early = tuple(range(3 * quarter, count))
    late = far + beside
    cross = functools.partial(swap, axis="lo", mask=1 << top_bit)

    pairs, early_part, near_part, *late_parts = first(
        (early, (0,) + near) + tuple((d,) for d in late),
        piece_rows,
        col_bits,
        top_bit,
        amplitudes,
        gates,
        phases,
        angles,
        bits,
        coupled,
        layout,
        pair,
    )
    early_other = cross(early_part)
    late_parts = [swap(part, "hi", d) for part, d in zip(late_parts, late, strict=True)]
    near_other = cross(near_part)
    sets = ((0,) + near + early[:-1], late + early[-1:])
    *turns, coefficients = second_phases(
        sets, piece_rows, rows, col_bits, after(phases, early_part), angles, bits, coupled, pair
    )
    early_other = after(early_other, coefficients)
    early_parts = combine(len(early), early_part, early_other, pairs, COMBINE_COST)
    early_parts = [swap(part, "hi", d) for part, d in zip(early_parts, early, strict=True)]
    own_part, *near_parts = combine(1 + len(near), near_part, near_other, pairs, 1000)
    late_part = joined([after(part, own_part) for part in late_parts], LATE_COST)
    late_other = cross(late_part)
    near_parts = [swap(part, "hi", d) for part, d in zip(near_parts, near, strict=True)]
    half_part = joined(early_parts[:-1], HALF_COST)
    near_turned = turned_pieces(
        turns[:2], [own_part] + [after(part, half_part) for part in near_parts] + [half_part]
    )
    near_turned_other = swap(near_turned, "lo", 1)
    parts = second_gates(sets, piece_rows, after(gates, near_turned))
    late_turned = turned(
        turns[2:], pairs, late_part, after(late_other, parts[0]), early_parts[-1]
    )
    late_turned_other = swap(late_turned, "lo", 1)
    total = middle(parts[:2], coefficients, near_turned, near_turned_other)
    return last(parts[2:], coefficients, late_turned, late_turned_other, total)


def solution(mesh):
    placed = (
        P(None, ("hi", "lo"), None, None),
        P(),
        P(),
        P(None, ("hi", "lo")),
        P(),
        P(),
        P(),
        P(),
    )
    return jax.shard_map(
        shards,
        mesh=mesh,
        in_specs=placed,
        out_specs=P(None, ("hi", "lo"), None, None),
        check_vma=False,
    )
```

```python
import functools

import jax
import jax.numpy as jnp
from jax import lax
from jax.experimental import pallas as pl
from jax.experimental.pallas import tpu as pltpu
from jax.sharding import PartitionSpec as P

F32 = jnp.float32
BF16 = jnp.bfloat16
VMEM_BYTES = 32 * 1024 * 1024
MIDDLE_COST = 3000000000
HALF_COST = 1000
CHUNKS = 2
LAST_CHUNKS = 4
COMBINE_COST = 1500001000
LATE_COST = 1000


def sincos(x):
    turns = jnp.floor(x * 0.6366197723675814 + 0.5)
    r = x - turns * 1.5703125
    r = r - turns * 4.837512969970703125e-4
    r = r - turns * 7.54978995489188216e-8
    z = r * r
    sine = r + r * z * ((-1.9515295891e-4 * z + 8.3321608736e-3) * z - 1.6666654611e-1)
    cosine = 1.0 - 0.5 * z + z * z * (
        (2.443315711809948e-5 * z - 1.388731625493765e-3) * z + 4.166664568298827e-2
    )
    quarter = turns.astype(jnp.int32) & 3
    odd = (quarter & 1) == 1
    new_sine = jnp.where(odd, cosine, sine)
    new_cosine = jnp.where(odd, sine, cosine)
    new_sine = jnp.where((quarter & 2) == 2, -new_sine, new_sine)
    new_cosine = jnp.where(((quarter + 1) & 2) == 2, -new_cosine, new_cosine)
    return new_cosine, new_sine


def qubit_factors(layer, phases_ref, bits_ref, coupled_ref):
    qubits = phases_ref.shape[1]
    lane = lax.broadcasted_iota(jnp.int32, (1, qubits), 1)
    odd = jnp.zeros((1, qubits), jnp.int32)
    for f in range(bits_ref.shape[0]):
        odd = odd ^ jnp.where(lane == coupled_ref[layer, f], bits_ref[f], 0)
    sign = 1.0 - 2.0 * odd.astype(F32)
    cosine, sine = sincos(phases_ref[layer : layer + 1, :])
    return cosine * sign, sine * sign


def turn(real, imag, cosine, sine):
    return real * cosine - imag * sine, real * sine + imag * cosine


def row_phases(cosine, sine, first, row_bits, base_real, base_imag):
    sub = lax.broadcasted_iota(jnp.int32, (8, 128), 0)
    real = jnp.broadcast_to(base_real, (8, 128))
    imag = jnp.broadcast_to(base_imag, (8, 128))
    for k in range(row_bits):
        c = cosine[:, first + k : first + k + 1]
        s = sine[:, first + k : first + k + 1]
        if k < 3:
            chosen = ((sub >> k) & 1) == 1
            real, imag = turn(real, imag, jnp.where(chosen, c, 1.0), jnp.where(chosen, s, 0.0))
        else:
            up_real, up_imag = turn(real, imag, c, s)
            real = jnp.concatenate([real, up_real], axis=0)
            imag = jnp.concatenate([imag, up_imag], axis=0)
    return real, imag


def col_phases(cosine, sine, col_bits, cols):
    lane = lax.broadcasted_iota(jnp.int32, (1, cols), 1)
    real = jnp.ones((1, cols), F32)
    imag = jnp.zeros((1, cols), F32)
    for k in range(col_bits):
        chosen = ((lane >> k) & 1) == 1
        c = cosine[:, k : k + 1]
        s = sine[:, k : k + 1]
        real, imag = turn(real, imag, jnp.where(chosen, c, 1.0), jnp.where(chosen, s, 0.0))
    return real, imag


def split(x):
    high = x.astype(BF16)
    low = (x - high.astype(F32)).astype(BF16)
    return high, low


def dot(a, b):
    return jnp.dot(a, b, preferred_element_type=F32)


def signed_block(r, i):
    return jnp.concatenate(
        [jnp.concatenate([r, i], axis=1), jnp.concatenate([-i, r], axis=1)], axis=0
    )


def turned_rows(real, imag, phase_real, phase_imag):
    reps = real.shape[1] // phase_real.shape[1]
    phase_real = jnp.concatenate([phase_real] * reps, axis=1)
    phase_imag = jnp.concatenate([phase_imag] * reps, axis=1)
    real, imag = turn(real, imag, phase_real, phase_imag)
    real_high, real_low = split(real)
    imag_high, imag_low = split(imag)
    return signed_block(real_high, imag_high), signed_block(real_low, imag_low)


def product(left_high, left_low, right_high, right_low):
    return dot(left_high, right_high) + dot(left_high, right_low) + dot(left_low, right_high)


def hbm(array):
    return pltpu.with_memory_space_constraint(array, pltpu.HBM)


def any_space():
    return pl.BlockSpec(memory_space=pl.ANY)


def smem():
    return pl.BlockSpec(memory_space=pltpu.SMEM)


def vmem():
    return pl.BlockSpec(memory_space=pltpu.VMEM)


def cost(flops=1000):
    return pl.CostEstimate(flops=flops, bytes_accessed=1000, transcendentals=0)


def params():
    return pltpu.CompilerParams(vmem_limit_bytes=VMEM_BYTES)


def chosen_rows(steps, piece_rows, rows, layout_ref):
    me = lax.axis_index("hi")
    row_bits = rows.bit_length() - 1
    sub = lax.broadcasted_iota(jnp.int32, (8, 128), 0)
    inner = jnp.zeros((8, 128), jnp.int32)
    inner_bits = piece_rows.bit_length() - 1
    for k in range(inner_bits):
        place = jnp.left_shift(jnp.int32(1), layout_ref[k])
        if k < 3:
            inner = inner + ((sub >> k) & 1) * place
        else:
            inner = jnp.concatenate([inner, inner + place], axis=0)
    places = []
    for step in steps:
        block = me ^ step
        base = jnp.int32(0)
        for k in range(inner_bits, row_bits):
            base = base + jnp.left_shift((block >> (k - inner_bits)) & 1, layout_ref[k])
        places.append(inner + base)
    places = jnp.concatenate(places, axis=0)
    lane = lax.broadcasted_iota(jnp.int32, places.shape, 1)
    return jnp.concatenate(
        [
            jnp.where(places == lane + start, 1.0, 0.0).astype(BF16)
            for start in range(0, rows, 128)
        ],
        axis=1,
    )


def first_kernel(
    groups,
    piece_rows,
    col_bits,
    top_bit,
    amplitudes_hbm,
    gates_hbm,
    phases_hbm,
    angles_hbm,
    bits_hbm,
    coupled_hbm,
    layout_hbm,
    pair_hbm,
    *refs,
):
    (
        pairs_ref,
        *out_refs,
        amplitudes_ref,
        gates_ref,
        phases_ref,
        angles_ref,
        bits_ref,
        coupled_ref,
        layout_ref,
        pair_ref,
        small_sems,
        chunk_sems,
    ) = refs
    rows, cols = amplitudes_ref.shape[2:]
    row_bits = rows.bit_length() - 1
    small = [
        pltpu.make_async_copy(source, target, small_sems.at[i])
        for i, (source, target) in enumerate(
            (
                (phases_hbm, phases_ref),
                (angles_hbm, angles_ref),
                (bits_hbm, bits_ref),
                (coupled_hbm, coupled_ref),
                (layout_hbm, layout_ref),
                (pair_hbm, pair_ref),
            )
        )
    ]
    count = chunk_sems.shape[0]
    step = rows // count
    chunks = []
    for k in range(count):
        part = pl.ds(k * step, step)
        chunks.append(
            [
                pltpu.make_async_copy(
                    gates_hbm.at[0, 0, :, part], gates_ref.at[0, :, part], chunk_sems.at[k, 0]
                ),
                pltpu.make_async_copy(
                    gates_hbm.at[0, 1, :, part], gates_ref.at[1, :, part], chunk_sems.at[k, 1]
                ),
                pltpu.make_async_copy(
                    amplitudes_hbm.at[:, :, part], amplitudes_ref.at[:, :, part], chunk_sems.at[k, 2]
                ),
            ]
        )
    for copy in small:
        copy.start()
    for chunk in chunks:
        for copy in chunk:
            copy.start()
    for copy in small:
        copy.wait()
    bit = (lax.axis_index("lo") >> top_bit) & 1
    c = pair_coefficients(pair_ref, 0, bit)
    for i in range(4):
        pairs_ref[i : i + 1, :] = jnp.full((1, cols), c[i], F32)
    pairs_ref[4:8, :] = jnp.zeros((4, cols), F32)
    cosine, sine = qubit_factors(0, phases_ref, bits_ref, coupled_ref)
    base_real, base_imag = sincos(angles_ref[0:1, 0:1])
    phase_real, phase_imag = row_phases(cosine, sine, col_bits, row_bits, base_real, base_imag)
    steps = [d for group in groups for d in group]
    chosen = chosen_rows(steps, piece_rows, rows, layout_ref)
    gated = None
    for k in range(count):
        for copy in chunks[k]:
            copy.wait()
        part = slice(k * step, (k + 1) * step)
        real_high, real_low = split(gates_ref[0, :, part])
        imag_high, imag_low = split(gates_ref[1, :, part])
        right_high, right_low = turned_rows(
            amplitudes_ref[0, 0, part], amplitudes_ref[1, 0, part], phase_real[part], phase_imag[part]
        )
        term = product(
            jnp.concatenate([real_high, imag_high], axis=1),
            jnp.concatenate([real_low, imag_low], axis=1),
            right_high,
            right_low,
        )
        gated = term if gated is None else gated + term
    gated_high, gated_low = split(gated)
    out = dot(chosen, gated_high) + dot(chosen, gated_low)
    start = 0
    for group, out_ref in zip(groups, out_refs, strict=True):
        size = len(group) * piece_rows
        out_ref[0] = out[start : start + size, :cols]
        out_ref[1] = out[start : start + size, cols:]
        start += size


def first(
    groups, piece_rows, col_bits, top_bit, amplitudes, gates, phases, angles, bits, coupled, layout, pair
):
    rows, cols = amplitudes.shape[2:]
    shapes = [jax.ShapeDtypeStruct((8, cols), F32)]
    shapes += [jax.ShapeDtypeStruct((2, len(group) * piece_rows, cols), F32) for group in groups]
    sources = (amplitudes, gates, phases, angles, bits, coupled, layout, pair)
    return pl.pallas_call(
        functools.partial(first_kernel, groups, piece_rows, col_bits, top_bit),
        out_shape=shapes,
        in_specs=[any_space()] * len(sources),
        out_specs=[vmem()] * len(shapes),
        scratch_shapes=[
            pltpu.VMEM(amplitudes.shape, F32),
            pltpu.VMEM(gates.shape[1:], F32),
            pltpu.VMEM(phases.shape, F32),
            pltpu.VMEM(angles.shape, F32),
            pltpu.SMEM(bits.shape, jnp.int32),
            pltpu.SMEM(coupled.shape, jnp.int32),
            pltpu.SMEM(layout.shape, jnp.int32),
            pltpu.SMEM(pair.shape, F32),
            pltpu.SemaphoreType.DMA((6,)),
            pltpu.SemaphoreType.DMA((CHUNKS, 3)),
        ],
        compiler_params=params(),
        cost_estimate=cost(),
        name="first",
    )(*[hbm(source) for source in sources])


def own_order(tile, piece_rows, me):
    lane = lax.broadcasted_iota(jnp.int32, tile.shape, 1)
    width = tile.shape[1]
    size = piece_rows
    bit = 0
    while size < width:
        upper = (lane & size) != 0
        swapped = jnp.where(
            upper, pltpu.roll(tile, size, 1), pltpu.roll(tile, width - size, 1)
        )
        tile = jnp.where(((me >> bit) & 1) == 1, swapped, tile)
        size *= 2
        bit += 1
    return tile


def phases_kernel(
    sets, piece_rows, col_bits, phases_ref, angles_ref, bits_ref, coupled_ref, pair_ref, *refs
):
    *out_refs, coefficients_ref, phase_real_ref, phase_imag_ref = refs
    me = lax.axis_index("hi")
    rows = phase_real_ref.shape[0]
    cols = coefficients_ref.shape[1]
    row_bits = rows.bit_length() - 1
    bit = lax.axis_index("lo") & 1
    before = qubit_factors(0, phases_ref, bits_ref, coupled_ref)
    after = qubit_factors(1, phases_ref, bits_ref, coupled_ref)
    base_real, base_imag = sincos(angles_ref[0:1, 1:2])
    phase_real_ref[...], phase_imag_ref[...] = row_phases(
        *after, col_bits, row_bits, base_real, base_imag
    )
    phase_real, phase_imag = turn(
        *col_phases(*before, col_bits, cols), *col_phases(*after, col_bits, cols)
    )
    c = pair_coefficients(pair_ref, 1, bit)
    c = turn(phase_real, phase_imag, c[0], c[1]) + turn(phase_real, phase_imag, c[2], c[3])
    for i in range(4):
        coefficients_ref[i : i + 1, :] = c[i]
    coefficients_ref[4:8, :] = jnp.zeros((4, cols), F32)
    for k, steps in enumerate(sets):
        for j, d in enumerate(steps):
            start = pl.multiple_of((me ^ d) * piece_rows, piece_rows)
            target = slice(j * piece_rows, (j + 1) * piece_rows)
            out_refs[2 * k][target, :] = phase_real_ref[pl.ds(start, piece_rows), :]
            out_refs[2 * k + 1][target, :] = phase_imag_ref[pl.ds(start, piece_rows), :]


def second_phases(sets, piece_rows, rows, col_bits, phases, angles, bits, coupled, pair):
    cols = 1 << col_bits
    shapes = []
    for steps in sets:
        shapes += [jax.ShapeDtypeStruct((len(steps) * piece_rows, 128), F32)] * 2
    shapes.append(jax.ShapeDtypeStruct((8, cols), F32))
    return pl.pallas_call(
        functools.partial(phases_kernel, sets, piece_rows, col_bits),
        out_shape=shapes,
        in_specs=[vmem(), vmem(), smem(), smem(), smem()],
        out_specs=[vmem()] * len(shapes),
        scratch_shapes=[pltpu.VMEM((rows, 128), F32)] * 2,
        compiler_params=params(),
        cost_estimate=cost(),
        name="second_phases",
    )(phases, angles, bits, coupled, pair)


def gates_kernel(sets, piece_rows, gates_hbm, *refs):
    *out_refs, gates_ref, sem = refs
    copy = pltpu.make_async_copy(gates_hbm.at[1], gates_ref, sem)
    copy.start()
    me = lax.axis_index("hi")
    size = gates_ref.shape[1] // 4
    quarter = size // piece_rows
    copy.wait()
    high, low = [], []
    for i in range(2):
        high_tiles, low_tiles = [], []
        for q in range(4):
            start = pl.multiple_of(((me // quarter) ^ q) * size, size)
            tile = own_order(gates_ref[i, :, pl.ds(start, size)], piece_rows, me)
            for tiles, part in zip((high_tiles, low_tiles), split(tile), strict=True):
                tiles.append(part)
        high.append(jnp.concatenate(high_tiles, axis=1))
        low.append(jnp.concatenate(low_tiles, axis=1))
    for k, steps in enumerate(sets):
        for part, out_ref in zip((high, low), out_refs[2 * k : 2 * k + 2], strict=True):
            out_ref[...] = jnp.concatenate(
                [
                    part[i][:, d * piece_rows : (d + 1) * piece_rows]
                    for i in range(2)
                    for d in steps
                ],
                axis=1,
            )


def second_gates(sets, piece_rows, gates):
    rows = gates.shape[2]
    shapes = []
    for steps in sets:
        shapes += [jax.ShapeDtypeStruct((rows, 2 * len(steps) * piece_rows), BF16)] * 2
    return pl.pallas_call(
        functools.partial(gates_kernel, sets, piece_rows),
        out_shape=shapes,
        in_specs=[any_space()],
        out_specs=[vmem()] * len(shapes),
        scratch_shapes=[pltpu.VMEM(gates.shape[1:], F32), pltpu.SemaphoreType.DMA],
        compiler_params=params(),
        cost_estimate=cost(),
        name="second_gates",
    )(hbm(gates))


def pair_coefficients(pair_ref, layer, bit):
    own = bit
    other = 1 - bit
    return (
        pair_ref[layer, 0, own, own],
        pair_ref[layer, 1, own, own],
        pair_ref[layer, 0, own, other],
        pair_ref[layer, 1, own, other],
    )


def combined(own, other, c):
    own_real, own_imag = turn(own[0], own[1], c[0], c[1])
    other_real, other_imag = turn(other[0], other[1], c[2], c[3])
    return own_real + other_real, own_imag + other_imag


def vector_coefficients(ref):
    return [ref[i : i + 1, :] for i in range(4)]


def combine_kernel(pairs_ref, own_ref, other_ref, *out_refs):
    c = vector_coefficients(pairs_ref)
    size = out_refs[0].shape[1]
    for i, out_ref in enumerate(out_refs):
        rows = slice(i * size, (i + 1) * size)
        out_ref[0], out_ref[1] = combined(
            (own_ref[0, rows], own_ref[1, rows]), (other_ref[0, rows], other_ref[1, rows]), c
        )


def combine(count, own, other, pairs, flops):
    shape = (2, own.shape[1] // count, own.shape[2])
    return pl.pallas_call(
        combine_kernel,
        out_shape=[jax.ShapeDtypeStruct(shape, F32)] * count,
        in_specs=[vmem()] * 3,
        out_specs=[vmem()] * count,
        compiler_params=params(),
        cost_estimate=cost(flops),
        name="combine",
    )(pairs, own, other)


def late_kernel(*refs):
    *part_refs, out_ref = refs
    size = part_refs[0].shape[1]
    for i, part_ref in enumerate(part_refs):
        out_ref[:, i * size : (i + 1) * size, :] = part_ref[...]


def joined(arrays, flops):
    _, size, cols = arrays[0].shape
    return pl.pallas_call(
        late_kernel,
        out_shape=jax.ShapeDtypeStruct((2, size * len(arrays), cols), F32),
        in_specs=[vmem()] * len(arrays),
        out_specs=vmem(),
        compiler_params=params(),
        cost_estimate=cost(flops),
        name="joined",
    )(*arrays)


def turned_pieces_kernel(phase_real_ref, phase_imag_ref, *refs):
    *piece_refs, out_ref = refs
    reps = out_ref.shape[2] // phase_real_ref.shape[1]
    start = 0
    for ref in piece_refs:
        part = slice(start, start + ref.shape[1])
        cosine = jnp.concatenate([phase_real_ref[part, :]] * reps, axis=1)
        sine = jnp.concatenate([phase_imag_ref[part, :]] * reps, axis=1)
        out_ref[0, part], out_ref[1, part] = turn(ref[0], ref[1], cosine, sine)
        start += ref.shape[1]


def turned_pieces(phase_parts, arrays):
    shape = (2, sum(a.shape[1] for a in arrays), arrays[0].shape[2])
    return pl.pallas_call(
        turned_pieces_kernel,
        out_shape=jax.ShapeDtypeStruct(shape, F32),
        in_specs=[vmem()] * (2 + len(arrays)),
        out_specs=vmem(),
        compiler_params=params(),
        cost_estimate=cost(MIDDLE_COST),
        name="turned_pieces",
    )(*phase_parts, *arrays)


def mixed_parts(coefficients_ref, own_ref, other_ref):
    c = vector_coefficients(coefficients_ref)
    real, imag = combined(own_ref, other_ref, c)
    real_high, real_low = split(real)
    imag_high, imag_low = split(imag)
    return signed_block(real_high, imag_high), signed_block(real_low, imag_low)


def middle_kernel(high_ref, low_ref, coefficients_ref, own_ref, other_ref, out_ref):
    cols = out_ref.shape[2]
    right_high, right_low = mixed_parts(coefficients_ref, own_ref, other_ref)
    out = product(high_ref[...], low_ref[...], right_high, right_low)
    out_ref[0] = out[:, :cols]
    out_ref[1] = out[:, cols:]


def middle(parts, coefficients, own, other):
    return pl.pallas_call(
        middle_kernel,
        out_shape=jax.ShapeDtypeStruct((2, parts[0].shape[0], own.shape[2]), F32),
        in_specs=[vmem()] * 5,
        out_specs=vmem(),
        compiler_params=params(),
        cost_estimate=cost(),
        name="middle",
    )(*parts, coefficients, own, other)


def turned_kernel(
    phase_real_ref, phase_imag_ref, pairs_ref, own_ref, other_ref, last_ref, out_ref
):
    size = own_ref.shape[1]
    parts = (
        (slice(0, size), combined(own_ref, other_ref, vector_coefficients(pairs_ref))),
        (slice(size, out_ref.shape[1]), (last_ref[0], last_ref[1])),
    )
    reps = out_ref.shape[2] // phase_real_ref.shape[1]
    for part, (real, imag) in parts:
        cosine = jnp.concatenate([phase_real_ref[part, :]] * reps, axis=1)
        sine = jnp.concatenate([phase_imag_ref[part, :]] * reps, axis=1)
        out_ref[0, part], out_ref[1, part] = turn(real, imag, cosine, sine)


def turned(phase_parts, pairs, own, other, last):
    shape = (2, own.shape[1] + last.shape[1], own.shape[2])
    return pl.pallas_call(
        turned_kernel,
        out_shape=jax.ShapeDtypeStruct(shape, F32),
        in_specs=[vmem()] * 6,
        out_specs=vmem(),
        compiler_params=params(),
        cost_estimate=cost(),
        name="turned",
    )(*phase_parts, pairs, own, other, last)


def last_kernel(
    high_ref, low_ref, coefficients_ref, own_ref, other_ref, sum_ref, out_hbm, out_ref, sems
):
    cols = own_ref.shape[2]
    right_high, right_low = mixed_parts(coefficients_ref, own_ref, other_ref)
    count = sems.shape[0]
    step = out_ref.shape[2] // count
    copies = []
    for i in range(count):
        part = pl.ds(i * step, step)
        out = product(high_ref[part, :], low_ref[part, :], right_high, right_low)
        out_ref[0, 0, part] = sum_ref[0, part] + out[:, :cols]
        out_ref[1, 0, part] = sum_ref[1, part] + out[:, cols:]
        copies.append(
            pltpu.make_async_copy(
                out_ref.at[:, :, part], out_hbm.at[:, :, part], sems.at[i]
            )
        )
        copies[-1].start()
    for copy in copies:
        copy.wait()


def last(parts, coefficients, own, other, total):
    _, rows, cols = total.shape
    shape = (2, 1, rows, cols)
    return pl.pallas_call(
        last_kernel,
        out_shape=jax.ShapeDtypeStruct(shape, F32),
        in_specs=[vmem()] * 6,
        out_specs=any_space(),
        scratch_shapes=[pltpu.VMEM(shape, F32), pltpu.SemaphoreType.DMA((LAST_CHUNKS,))],
        compiler_params=params(),
        cost_estimate=cost(),
        name="last",
    )(*parts, coefficients, own, other, total)


def swap(value, axis, mask):
    return lax.ppermute(value, axis, [(i, i ^ mask) for i in range(lax.axis_size(axis))])


def after(value, earlier):
    return lax.optimization_barrier((value, earlier))[0]


def shards(amplitudes, gates, pair, angles, phases, bits, coupled, layout):
    rows = amplitudes.shape[2]
    cols = amplitudes.shape[3]
    col_bits = cols.bit_length() - 1
    count = lax.axis_size("hi")
    piece_rows = rows // count
    top_bit = lax.axis_size("lo").bit_length() - 2
    quarter = count // 4
    angles = angles.T
    beside = tuple(range(1, quarter))
    near = tuple(range(quarter, 2 * quarter))
    far = tuple(range(2 * quarter, 3 * quarter))
    early = tuple(reversed(range(3 * quarter, count)))
    late = far + beside
    cross = functools.partial(swap, axis="lo", mask=1 << top_bit)

    pairs, early_part, near_part, *late_parts = first(
        (early, (0,) + near) + tuple((d,) for d in late),
        piece_rows,
        col_bits,
        top_bit,
        amplitudes,
        gates,
        phases,
        angles,
        bits,
        coupled,
        layout,
        pair,
    )
    early_other = cross(early_part)
    late_parts = [swap(part, "hi", d) for part, d in zip(late_parts, late, strict=True)]
    near_other = cross(near_part)
    sets = ((0,) + near + early[:-1], late + early[-1:])
    *turns, coefficients = second_phases(
        sets, piece_rows, rows, col_bits, after(phases, early_part), angles, bits, coupled, pair
    )
    early_other = after(early_other, coefficients)
    early_parts = combine(len(early), early_part, early_other, pairs, COMBINE_COST)
    early_parts = [swap(part, "hi", d) for part, d in zip(early_parts, early, strict=True)]
    own_part, *near_parts = combine(1 + len(near), near_part, near_other, pairs, 1000)
    late_part = joined([after(part, own_part) for part in late_parts], LATE_COST)
    late_other = cross(late_part)
    near_parts = [swap(part, "hi", d) for part, d in zip(near_parts, near, strict=True)]
    half_part = joined(early_parts[:-1], HALF_COST)
    near_turned = turned_pieces(
        turns[:2], [own_part] + [after(part, half_part) for part in near_parts] + [half_part]
    )
    near_turned_other = swap(near_turned, "lo", 1)
    parts = second_gates(sets, piece_rows, after(gates, near_turned))
    late_turned = turned(
        turns[2:], pairs, late_part, after(late_other, parts[0]), early_parts[-1]
    )
    late_turned_other = swap(late_turned, "lo", 1)
    total = middle(parts[:2], coefficients, near_turned, near_turned_other)
    return last(parts[2:], coefficients, late_turned, late_turned_other, total)


def solution(mesh):
    placed = (
        P(None, ("hi", "lo"), None, None),
        P(),
        P(),
        P(None, ("hi", "lo")),
        P(),
        P(),
        P(),
        P(),
    )
    return jax.shard_map(
        shards,
        mesh=mesh,
        in_specs=placed,
        out_specs=P(None, ("hi", "lo"), None, None),
        check_vma=False,
    )
```

```python
import functools

import jax
import jax.numpy as jnp
from jax import lax
from jax.experimental import pallas as pl
from jax.experimental.pallas import tpu as pltpu
from jax.sharding import PartitionSpec as P

F32 = jnp.float32
BF16 = jnp.bfloat16
VMEM_BYTES = 32 * 1024 * 1024
MIDDLE_COST = 3000000000
HALF_COST = 1000
CHUNKS = 2
LAST_PARTS = (2, 1, 1)
COMBINE_COST = 1500001000
LATE_COST = 1000


def sincos(x):
    turns = jnp.floor(x * 0.6366197723675814 + 0.5)
    r = x - turns * 1.5703125
    r = r - turns * 4.837512969970703125e-4
    r = r - turns * 7.54978995489188216e-8
    z = r * r
    sine = r + r * z * ((-1.9515295891e-4 * z + 8.3321608736e-3) * z - 1.6666654611e-1)
    cosine = 1.0 - 0.5 * z + z * z * (
        (2.443315711809948e-5 * z - 1.388731625493765e-3) * z + 4.166664568298827e-2
    )
    quarter = turns.astype(jnp.int32) & 3
    odd = (quarter & 1) == 1
    new_sine = jnp.where(odd, cosine, sine)
    new_cosine = jnp.where(odd, sine, cosine)
    new_sine = jnp.where((quarter & 2) == 2, -new_sine, new_sine)
    new_cosine = jnp.where(((quarter + 1) & 2) == 2, -new_cosine, new_cosine)
    return new_cosine, new_sine


def qubit_factors(layer, phases_ref, bits_ref, coupled_ref):
    qubits = phases_ref.shape[1]
    lane = lax.broadcasted_iota(jnp.int32, (1, qubits), 1)
    odd = jnp.zeros((1, qubits), jnp.int32)
    for f in range(bits_ref.shape[0]):
        odd = odd ^ jnp.where(lane == coupled_ref[layer, f], bits_ref[f], 0)
    sign = 1.0 - 2.0 * odd.astype(F32)
    cosine, sine = sincos(phases_ref[layer : layer + 1, :])
    return cosine * sign, sine * sign


def turn(real, imag, cosine, sine):
    return real * cosine - imag * sine, real * sine + imag * cosine


def row_phases(cosine, sine, first, row_bits, base_real, base_imag):
    sub = lax.broadcasted_iota(jnp.int32, (8, 128), 0)
    real = jnp.broadcast_to(base_real, (8, 128))
    imag = jnp.broadcast_to(base_imag, (8, 128))
    for k in range(row_bits):
        c = cosine[:, first + k : first + k + 1]
        s = sine[:, first + k : first + k + 1]
        if k < 3:
            chosen = ((sub >> k) & 1) == 1
            real, imag = turn(real, imag, jnp.where(chosen, c, 1.0), jnp.where(chosen, s, 0.0))
        else:
            up_real, up_imag = turn(real, imag, c, s)
            real = jnp.concatenate([real, up_real], axis=0)
            imag = jnp.concatenate([imag, up_imag], axis=0)
    return real, imag


def col_phases(cosine, sine, col_bits, cols):
    lane = lax.broadcasted_iota(jnp.int32, (1, cols), 1)
    real = jnp.ones((1, cols), F32)
    imag = jnp.zeros((1, cols), F32)
    for k in range(col_bits):
        chosen = ((lane >> k) & 1) == 1
        c = cosine[:, k : k + 1]
        s = sine[:, k : k + 1]
        real, imag = turn(real, imag, jnp.where(chosen, c, 1.0), jnp.where(chosen, s, 0.0))
    return real, imag


def split(x):
    high = x.astype(BF16)
    low = (x - high.astype(F32)).astype(BF16)
    return high, low


def dot(a, b):
    return jnp.dot(a, b, preferred_element_type=F32)


def signed_block(r, i):
    return jnp.concatenate(
        [jnp.concatenate([r, i], axis=1), jnp.concatenate([-i, r], axis=1)], axis=0
    )


def turned_rows(real, imag, phase_real, phase_imag):
    reps = real.shape[1] // phase_real.shape[1]
    phase_real = jnp.concatenate([phase_real] * reps, axis=1)
    phase_imag = jnp.concatenate([phase_imag] * reps, axis=1)
    real, imag = turn(real, imag, phase_real, phase_imag)
    real_high, real_low = split(real)
    imag_high, imag_low = split(imag)
    return signed_block(real_high, imag_high), signed_block(real_low, imag_low)


def product(left_high, left_low, right_high, right_low):
    return dot(left_high, right_high) + dot(left_high, right_low) + dot(left_low, right_high)


def hbm(array):
    return pltpu.with_memory_space_constraint(array, pltpu.HBM)


def any_space():
    return pl.BlockSpec(memory_space=pl.ANY)


def smem():
    return pl.BlockSpec(memory_space=pltpu.SMEM)


def vmem():
    return pl.BlockSpec(memory_space=pltpu.VMEM)


def cost(flops=1000):
    return pl.CostEstimate(flops=flops, bytes_accessed=1000, transcendentals=0)


def params():
    return pltpu.CompilerParams(vmem_limit_bytes=VMEM_BYTES)


def chosen_rows(steps, piece_rows, rows, layout_ref):
    me = lax.axis_index("hi")
    row_bits = rows.bit_length() - 1
    sub = lax.broadcasted_iota(jnp.int32, (8, 128), 0)
    inner = jnp.zeros((8, 128), jnp.int32)
    inner_bits = piece_rows.bit_length() - 1
    for k in range(inner_bits):
        place = jnp.left_shift(jnp.int32(1), layout_ref[k])
        if k < 3:
            inner = inner + ((sub >> k) & 1) * place
        else:
            inner = jnp.concatenate([inner, inner + place], axis=0)
    places = []
    for step in steps:
        block = me ^ step
        base = jnp.int32(0)
        for k in range(inner_bits, row_bits):
            base = base + jnp.left_shift((block >> (k - inner_bits)) & 1, layout_ref[k])
        places.append(inner + base)
    places = jnp.concatenate(places, axis=0)
    lane = lax.broadcasted_iota(jnp.int32, places.shape, 1)
    return jnp.concatenate(
        [
            jnp.where(places == lane + start, 1.0, 0.0).astype(BF16)
            for start in range(0, rows, 128)
        ],
        axis=1,
    )


def first_kernel(
    groups,
    piece_rows,
    col_bits,
    top_bit,
    amplitudes_hbm,
    gates_hbm,
    phases_hbm,
    angles_hbm,
    bits_hbm,
    coupled_hbm,
    layout_hbm,
    pair_hbm,
    *refs,
):
    (
        pairs_ref,
        *out_refs,
        amplitudes_ref,
        gates_ref,
        phases_ref,
        angles_ref,
        bits_ref,
        coupled_ref,
        layout_ref,
        pair_ref,
        small_sems,
        chunk_sems,
    ) = refs
    rows, cols = amplitudes_ref.shape[2:]
    row_bits = rows.bit_length() - 1
    small = [
        pltpu.make_async_copy(source, target, small_sems.at[i])
        for i, (source, target) in enumerate(
            (
                (phases_hbm, phases_ref),
                (angles_hbm, angles_ref),
                (bits_hbm, bits_ref),
                (coupled_hbm, coupled_ref),
                (layout_hbm, layout_ref),
                (pair_hbm, pair_ref),
            )
        )
    ]
    count = chunk_sems.shape[0]
    step = rows // count
    chunks = []
    for k in range(count):
        part = pl.ds(k * step, step)
        chunks.append(
            [
                pltpu.make_async_copy(
                    gates_hbm.at[0, 0, :, part], gates_ref.at[0, :, part], chunk_sems.at[k, 0]
                ),
                pltpu.make_async_copy(
                    gates_hbm.at[0, 1, :, part], gates_ref.at[1, :, part], chunk_sems.at[k, 1]
                ),
                pltpu.make_async_copy(
                    amplitudes_hbm.at[:, :, part], amplitudes_ref.at[:, :, part], chunk_sems.at[k, 2]
                ),
            ]
        )
    for copy in small:
        copy.start()
    for chunk in chunks:
        for copy in chunk:
            copy.start()
    for copy in small:
        copy.wait()
    bit = (lax.axis_index("lo") >> top_bit) & 1
    c = pair_coefficients(pair_ref, 0, bit)
    for i in range(4):
        pairs_ref[i : i + 1, :] = jnp.full((1, cols), c[i], F32)
    pairs_ref[4:8, :] = jnp.zeros((4, cols), F32)
    cosine, sine = qubit_factors(0, phases_ref, bits_ref, coupled_ref)
    base_real, base_imag = sincos(angles_ref[0:1, 0:1])
    phase_real, phase_imag = row_phases(cosine, sine, col_bits, row_bits, base_real, base_imag)
    steps = [d for group in groups for d in group]
    chosen = chosen_rows(steps, piece_rows, rows, layout_ref)
    gated = None
    for k in range(count):
        for copy in chunks[k]:
            copy.wait()
        part = slice(k * step, (k + 1) * step)
        real_high, real_low = split(gates_ref[0, :, part])
        imag_high, imag_low = split(gates_ref[1, :, part])
        right_high, right_low = turned_rows(
            amplitudes_ref[0, 0, part], amplitudes_ref[1, 0, part], phase_real[part], phase_imag[part]
        )
        term = product(
            jnp.concatenate([real_high, imag_high], axis=1),
            jnp.concatenate([real_low, imag_low], axis=1),
            right_high,
            right_low,
        )
        gated = term if gated is None else gated + term
    gated_high, gated_low = split(gated)
    out = dot(chosen, gated_high) + dot(chosen, gated_low)
    start = 0
    for group, out_ref in zip(groups, out_refs, strict=True):
        size = len(group) * piece_rows
        out_ref[0] = out[start : start + size, :cols]
        out_ref[1] = out[start : start + size, cols:]
        start += size


def first(
    groups, piece_rows, col_bits, top_bit, amplitudes, gates, phases, angles, bits, coupled, layout, pair
):
    rows, cols = amplitudes.shape[2:]
    shapes = [jax.ShapeDtypeStruct((8, cols), F32)]
    shapes += [jax.ShapeDtypeStruct((2, len(group) * piece_rows, cols), F32) for group in groups]
    sources = (amplitudes, gates, phases, angles, bits, coupled, layout, pair)
    return pl.pallas_call(
        functools.partial(first_kernel, groups, piece_rows, col_bits, top_bit),
        out_shape=shapes,
        in_specs=[any_space()] * len(sources),
        out_specs=[vmem()] * len(shapes),
        scratch_shapes=[
            pltpu.VMEM(amplitudes.shape, F32),
            pltpu.VMEM(gates.shape[1:], F32),
            pltpu.VMEM(phases.shape, F32),
            pltpu.VMEM(angles.shape, F32),
            pltpu.SMEM(bits.shape, jnp.int32),
            pltpu.SMEM(coupled.shape, jnp.int32),
            pltpu.SMEM(layout.shape, jnp.int32),
            pltpu.SMEM(pair.shape, F32),
            pltpu.SemaphoreType.DMA((6,)),
            pltpu.SemaphoreType.DMA((CHUNKS, 3)),
        ],
        compiler_params=params(),
        cost_estimate=cost(),
        name="first",
    )(*[hbm(source) for source in sources])


def own_order(tile, piece_rows, me):
    lane = lax.broadcasted_iota(jnp.int32, tile.shape, 1)
    width = tile.shape[1]
    size = piece_rows
    bit = 0
    while size < width:
        upper = (lane & size) != 0
        swapped = jnp.where(
            upper, pltpu.roll(tile, size, 1), pltpu.roll(tile, width - size, 1)
        )
        tile = jnp.where(((me >> bit) & 1) == 1, swapped, tile)
        size *= 2
        bit += 1
    return tile


def phases_kernel(
    sets, piece_rows, col_bits, phases_ref, angles_ref, bits_ref, coupled_ref, pair_ref, *refs
):
    *out_refs, coefficients_ref, phase_real_ref, phase_imag_ref = refs
    me = lax.axis_index("hi")
    rows = phase_real_ref.shape[0]
    cols = coefficients_ref.shape[1]
    row_bits = rows.bit_length() - 1
    bit = lax.axis_index("lo") & 1
    before = qubit_factors(0, phases_ref, bits_ref, coupled_ref)
    after = qubit_factors(1, phases_ref, bits_ref, coupled_ref)
    base_real, base_imag = sincos(angles_ref[0:1, 1:2])
    phase_real_ref[...], phase_imag_ref[...] = row_phases(
        *after, col_bits, row_bits, base_real, base_imag
    )
    phase_real, phase_imag = turn(
        *col_phases(*before, col_bits, cols), *col_phases(*after, col_bits, cols)
    )
    c = pair_coefficients(pair_ref, 1, bit)
    c = turn(phase_real, phase_imag, c[0], c[1]) + turn(phase_real, phase_imag, c[2], c[3])
    for i in range(4):
        coefficients_ref[i : i + 1, :] = c[i]
    coefficients_ref[4:8, :] = jnp.zeros((4, cols), F32)
    for k, steps in enumerate(sets):
        for j, d in enumerate(steps):
            start = pl.multiple_of((me ^ d) * piece_rows, piece_rows)
            target = slice(j * piece_rows, (j + 1) * piece_rows)
            out_refs[2 * k][target, :] = phase_real_ref[pl.ds(start, piece_rows), :]
            out_refs[2 * k + 1][target, :] = phase_imag_ref[pl.ds(start, piece_rows), :]


def second_phases(sets, piece_rows, rows, col_bits, phases, angles, bits, coupled, pair):
    cols = 1 << col_bits
    shapes = []
    for steps in sets:
        shapes += [jax.ShapeDtypeStruct((len(steps) * piece_rows, 128), F32)] * 2
    shapes.append(jax.ShapeDtypeStruct((8, cols), F32))
    return pl.pallas_call(
        functools.partial(phases_kernel, sets, piece_rows, col_bits),
        out_shape=shapes,
        in_specs=[vmem(), vmem(), smem(), smem(), smem()],
        out_specs=[vmem()] * len(shapes),
        scratch_shapes=[pltpu.VMEM((rows, 128), F32)] * 2,
        compiler_params=params(),
        cost_estimate=cost(),
        name="second_phases",
    )(phases, angles, bits, coupled, pair)


def gates_kernel(sets, piece_rows, gates_hbm, *refs):
    *out_refs, gates_ref, sem = refs
    copy = pltpu.make_async_copy(gates_hbm.at[1], gates_ref, sem)
    copy.start()
    me = lax.axis_index("hi")
    size = gates_ref.shape[1] // 4
    quarter = size // piece_rows
    copy.wait()
    high, low = [], []
    for i in range(2):
        high_tiles, low_tiles = [], []
        for q in range(4):
            start = pl.multiple_of(((me // quarter) ^ q) * size, size)
            tile = own_order(gates_ref[i, :, pl.ds(start, size)], piece_rows, me)
            for tiles, part in zip((high_tiles, low_tiles), split(tile), strict=True):
                tiles.append(part)
        high.append(jnp.concatenate(high_tiles, axis=1))
        low.append(jnp.concatenate(low_tiles, axis=1))
    for k, steps in enumerate(sets):
        for part, out_ref in zip((high, low), out_refs[2 * k : 2 * k + 2], strict=True):
            out_ref[...] = jnp.concatenate(
                [
                    part[i][:, d * piece_rows : (d + 1) * piece_rows]
                    for i in range(2)
                    for d in steps
                ],
                axis=1,
            )


def second_gates(sets, piece_rows, gates):
    rows = gates.shape[2]
    shapes = []
    for steps in sets:
        shapes += [jax.ShapeDtypeStruct((rows, 2 * len(steps) * piece_rows), BF16)] * 2
    return pl.pallas_call(
        functools.partial(gates_kernel, sets, piece_rows),
        out_shape=shapes,
        in_specs=[any_space()],
        out_specs=[vmem()] * len(shapes),
        scratch_shapes=[pltpu.VMEM(gates.shape[1:], F32), pltpu.SemaphoreType.DMA],
        compiler_params=params(),
        cost_estimate=cost(),
        name="second_gates",
    )(hbm(gates))


def pair_coefficients(pair_ref, layer, bit):
    own = bit
    other = 1 - bit
    return (
        pair_ref[layer, 0, own, own],
        pair_ref[layer, 1, own, own],
        pair_ref[layer, 0, own, other],
        pair_ref[layer, 1, own, other],
    )


def combined(own, other, c):
    own_real, own_imag = turn(own[0], own[1], c[0], c[1])
    other_real, other_imag = turn(other[0], other[1], c[2], c[3])
    return own_real + other_real, own_imag + other_imag


def vector_coefficients(ref):
    return [ref[i : i + 1, :] for i in range(4)]


def combine_kernel(pairs_ref, own_ref, other_ref, *out_refs):
    c = vector_coefficients(pairs_ref)
    size = out_refs[0].shape[1]
    for i, out_ref in enumerate(out_refs):
        rows = slice(i * size, (i + 1) * size)
        out_ref[0], out_ref[1] = combined(
            (own_ref[0, rows], own_ref[1, rows]), (other_ref[0, rows], other_ref[1, rows]), c
        )


def combine(count, own, other, pairs, flops):
    shape = (2, own.shape[1] // count, own.shape[2])
    return pl.pallas_call(
        combine_kernel,
        out_shape=[jax.ShapeDtypeStruct(shape, F32)] * count,
        in_specs=[vmem()] * 3,
        out_specs=[vmem()] * count,
        compiler_params=params(),
        cost_estimate=cost(flops),
        name="combine",
    )(pairs, own, other)


def late_kernel(*refs):
    *part_refs, out_ref = refs
    size = part_refs[0].shape[1]
    for i, part_ref in enumerate(part_refs):
        out_ref[:, i * size : (i + 1) * size, :] = part_ref[...]


def joined(arrays, flops):
    _, size, cols = arrays[0].shape
    return pl.pallas_call(
        late_kernel,
        out_shape=jax.ShapeDtypeStruct((2, size * len(arrays), cols), F32),
        in_specs=[vmem()] * len(arrays),
        out_specs=vmem(),
        compiler_params=params(),
        cost_estimate=cost(flops),
        name="joined",
    )(*arrays)


def turned_pieces_kernel(phase_real_ref, phase_imag_ref, *refs):
    *piece_refs, out_ref = refs
    reps = out_ref.shape[2] // phase_real_ref.shape[1]
    start = 0
    for ref in piece_refs:
        part = slice(start, start + ref.shape[1])
        cosine = jnp.concatenate([phase_real_ref[part, :]] * reps, axis=1)
        sine = jnp.concatenate([phase_imag_ref[part, :]] * reps, axis=1)
        out_ref[0, part], out_ref[1, part] = turn(ref[0], ref[1], cosine, sine)
        start += ref.shape[1]


def turned_pieces(phase_parts, arrays):
    shape = (2, sum(a.shape[1] for a in arrays), arrays[0].shape[2])
    return pl.pallas_call(
        turned_pieces_kernel,
        out_shape=jax.ShapeDtypeStruct(shape, F32),
        in_specs=[vmem()] * (2 + len(arrays)),
        out_specs=vmem(),
        compiler_params=params(),
        cost_estimate=cost(MIDDLE_COST),
        name="turned_pieces",
    )(*phase_parts, *arrays)


def mixed_parts(coefficients_ref, own_ref, other_ref):
    c = vector_coefficients(coefficients_ref)
    real, imag = combined(own_ref, other_ref, c)
    real_high, real_low = split(real)
    imag_high, imag_low = split(imag)
    return signed_block(real_high, imag_high), signed_block(real_low, imag_low)


def middle_kernel(high_ref, low_ref, coefficients_ref, own_ref, other_ref, out_ref):
    cols = out_ref.shape[2]
    right_high, right_low = mixed_parts(coefficients_ref, own_ref, other_ref)
    out = product(high_ref[...], low_ref[...], right_high, right_low)
    out_ref[0] = out[:, :cols]
    out_ref[1] = out[:, cols:]


def middle(parts, coefficients, own, other):
    return pl.pallas_call(
        middle_kernel,
        out_shape=jax.ShapeDtypeStruct((2, parts[0].shape[0], own.shape[2]), F32),
        in_specs=[vmem()] * 5,
        out_specs=vmem(),
        compiler_params=params(),
        cost_estimate=cost(),
        name="middle",
    )(*parts, coefficients, own, other)


def turned_kernel(
    phase_real_ref, phase_imag_ref, pairs_ref, own_ref, other_ref, last_ref, out_ref
):
    size = own_ref.shape[1]
    parts = (
        (slice(0, size), combined(own_ref, other_ref, vector_coefficients(pairs_ref))),
        (slice(size, out_ref.shape[1]), (last_ref[0], last_ref[1])),
    )
    reps = out_ref.shape[2] // phase_real_ref.shape[1]
    for part, (real, imag) in parts:
        cosine = jnp.concatenate([phase_real_ref[part, :]] * reps, axis=1)
        sine = jnp.concatenate([phase_imag_ref[part, :]] * reps, axis=1)
        out_ref[0, part], out_ref[1, part] = turn(real, imag, cosine, sine)


def turned(phase_parts, pairs, own, other, last):
    shape = (2, own.shape[1] + last.shape[1], own.shape[2])
    return pl.pallas_call(
        turned_kernel,
        out_shape=jax.ShapeDtypeStruct(shape, F32),
        in_specs=[vmem()] * 6,
        out_specs=vmem(),
        compiler_params=params(),
        cost_estimate=cost(),
        name="turned",
    )(*phase_parts, pairs, own, other, last)


def last_kernel(
    high_ref, low_ref, coefficients_ref, own_ref, other_ref, sum_ref, out_hbm, out_ref, sems
):
    cols = own_ref.shape[2]
    right_high, right_low = mixed_parts(coefficients_ref, own_ref, other_ref)
    unit = out_ref.shape[2] // sum(LAST_PARTS)
    copies = []
    start = 0
    for i, size in enumerate(LAST_PARTS):
        part = pl.ds(start, size * unit)
        start += size * unit
        out = product(high_ref[part, :], low_ref[part, :], right_high, right_low)
        out_ref[0, 0, part] = sum_ref[0, part] + out[:, :cols]
        out_ref[1, 0, part] = sum_ref[1, part] + out[:, cols:]
        copies.append(
            pltpu.make_async_copy(
                out_ref.at[:, :, part], out_hbm.at[:, :, part], sems.at[i]
            )
        )
        copies[-1].start()
    for copy in copies:
        copy.wait()


def last(parts, coefficients, own, other, total):
    _, rows, cols = total.shape
    shape = (2, 1, rows, cols)
    return pl.pallas_call(
        last_kernel,
        out_shape=jax.ShapeDtypeStruct(shape, F32),
        in_specs=[vmem()] * 6,
        out_specs=any_space(),
        scratch_shapes=[pltpu.VMEM(shape, F32), pltpu.SemaphoreType.DMA((len(LAST_PARTS),))],
        compiler_params=params(),
        cost_estimate=cost(),
        name="last",
    )(*parts, coefficients, own, other, total)


def swap(value, axis, mask):
    return lax.ppermute(value, axis, [(i, i ^ mask) for i in range(lax.axis_size(axis))])


def after(value, earlier):
    return lax.optimization_barrier((value, earlier))[0]


def shards(amplitudes, gates, pair, angles, phases, bits, coupled, layout):
    rows = amplitudes.shape[2]
    cols = amplitudes.shape[3]
    col_bits = cols.bit_length() - 1
    count = lax.axis_size("hi")
    piece_rows = rows // count
    top_bit = lax.axis_size("lo").bit_length() - 2
    quarter = count // 4
    angles = angles.T
    beside = tuple(range(1, quarter))
    near = tuple(range(quarter, 2 * quarter))
    far = tuple(range(2 * quarter, 3 * quarter))
    early = tuple(reversed(range(3 * quarter, count)))
    late = far + beside
    cross = functools.partial(swap, axis="lo", mask=1 << top_bit)

    pairs, early_part, near_part, *late_parts = first(
        (early, (0,) + near) + tuple((d,) for d in late),
        piece_rows,
        col_bits,
        top_bit,
        amplitudes,
        gates,
        phases,
        angles,
        bits,
        coupled,
        layout,
        pair,
    )
    early_other = cross(early_part)
    late_parts = [swap(part, "hi", d) for part, d in zip(late_parts, late, strict=True)]
    near_other = cross(near_part)
    sets = ((0,) + near + early[:-1], late + early[-1:])
    *turns, coefficients = second_phases(
        sets, piece_rows, rows, col_bits, after(phases, early_part), angles, bits, coupled, pair
    )
    early_other = after(early_other, coefficients)
    early_parts = combine(len(early), early_part, early_other, pairs, COMBINE_COST)
    early_parts = [swap(part, "hi", d) for part, d in zip(early_parts, early, strict=True)]
    own_part, *near_parts = combine(1 + len(near), near_part, near_other, pairs, 1000)
    late_part = joined([after(part, own_part) for part in late_parts], LATE_COST)
    late_other = cross(late_part)
    near_parts = [swap(part, "hi", d) for part, d in zip(near_parts, near, strict=True)]
    half_part = joined(early_parts[:-1], HALF_COST)
    near_turned = turned_pieces(
        turns[:2], [own_part] + [after(part, half_part) for part in near_parts] + [half_part]
    )
    near_turned_other = swap(near_turned, "lo", 1)
    parts = second_gates(sets, piece_rows, after(gates, near_turned))
    late_turned = turned(
        turns[2:], pairs, late_part, after(late_other, parts[0]), early_parts[-1]
    )
    late_turned_other = swap(late_turned, "lo", 1)
    total = middle(parts[:2], coefficients, near_turned, near_turned_other)
    return last(parts[2:], coefficients, late_turned, late_turned_other, total)


def solution(mesh):
    placed = (
        P(None, ("hi", "lo"), None, None),
        P(),
        P(),
        P(None, ("hi", "lo")),
        P(),
        P(),
        P(),
        P(),
    )
    return jax.shard_map(
        shards,
        mesh=mesh,
        in_specs=placed,
        out_specs=P(None, ("hi", "lo"), None, None),
        check_vma=False,
    )
```

```python
import functools

import jax
import jax.numpy as jnp
from jax import lax
from jax.experimental import pallas as pl
from jax.experimental.pallas import tpu as pltpu
from jax.sharding import PartitionSpec as P

F32 = jnp.float32
BF16 = jnp.bfloat16
VMEM_BYTES = 32 * 1024 * 1024
MIDDLE_COST = 3000000000
HALF_COST = 1000
CHUNKS = 2
LAST_PARTS = (2, 1, 1)
COMBINE_COST = 1500001000
LATE_COST = 1000


def sincos(x):
    turns = jnp.floor(x * 0.6366197723675814 + 0.5)
    r = x - turns * 1.5703125
    r = r - turns * 4.837512969970703125e-4
    r = r - turns * 7.54978995489188216e-8
    z = r * r
    sine = r + r * z * ((-1.9515295891e-4 * z + 8.3321608736e-3) * z - 1.6666654611e-1)
    cosine = 1.0 - 0.5 * z + z * z * (
        (2.443315711809948e-5 * z - 1.388731625493765e-3) * z + 4.166664568298827e-2
    )
    quarter = turns.astype(jnp.int32) & 3
    odd = (quarter & 1) == 1
    new_sine = jnp.where(odd, cosine, sine)
    new_cosine = jnp.where(odd, sine, cosine)
    new_sine = jnp.where((quarter & 2) == 2, -new_sine, new_sine)
    new_cosine = jnp.where(((quarter + 1) & 2) == 2, -new_cosine, new_cosine)
    return new_cosine, new_sine


def qubit_factors(layer, phases_ref, bits_ref, coupled_ref):
    qubits = phases_ref.shape[1]
    lane = lax.broadcasted_iota(jnp.int32, (1, qubits), 1)
    odd = jnp.zeros((1, qubits), jnp.int32)
    for f in range(bits_ref.shape[0]):
        odd = odd ^ jnp.where(lane == coupled_ref[layer, f], bits_ref[f], 0)
    sign = 1.0 - 2.0 * odd.astype(F32)
    cosine, sine = sincos(phases_ref[layer : layer + 1, :])
    return cosine * sign, sine * sign


def turn(real, imag, cosine, sine):
    return real * cosine - imag * sine, real * sine + imag * cosine


def row_phases(cosine, sine, first, row_bits, base_real, base_imag):
    sub = lax.broadcasted_iota(jnp.int32, (8, 128), 0)
    real = jnp.broadcast_to(base_real, (8, 128))
    imag = jnp.broadcast_to(base_imag, (8, 128))
    for k in range(row_bits):
        c = cosine[:, first + k : first + k + 1]
        s = sine[:, first + k : first + k + 1]
        if k < 3:
            chosen = ((sub >> k) & 1) == 1
            real, imag = turn(real, imag, jnp.where(chosen, c, 1.0), jnp.where(chosen, s, 0.0))
        else:
            up_real, up_imag = turn(real, imag, c, s)
            real = jnp.concatenate([real, up_real], axis=0)
            imag = jnp.concatenate([imag, up_imag], axis=0)
    return real, imag


def col_phases(cosine, sine, col_bits, cols):
    lane = lax.broadcasted_iota(jnp.int32, (1, cols), 1)
    real = jnp.ones((1, cols), F32)
    imag = jnp.zeros((1, cols), F32)
    for k in range(col_bits):
        chosen = ((lane >> k) & 1) == 1
        c = cosine[:, k : k + 1]
        s = sine[:, k : k + 1]
        real, imag = turn(real, imag, jnp.where(chosen, c, 1.0), jnp.where(chosen, s, 0.0))
    return real, imag


def split(x):
    high = x.astype(BF16)
    low = (x - high.astype(F32)).astype(BF16)
    return high, low


def dot(a, b):
    return jnp.dot(a, b, preferred_element_type=F32)


def signed_block(r, i):
    return jnp.concatenate(
        [jnp.concatenate([r, i], axis=1), jnp.concatenate([-i, r], axis=1)], axis=0
    )


def turned_rows(real, imag, phase_real, phase_imag):
    reps = real.shape[1] // phase_real.shape[1]
    phase_real = jnp.concatenate([phase_real] * reps, axis=1)
    phase_imag = jnp.concatenate([phase_imag] * reps, axis=1)
    real, imag = turn(real, imag, phase_real, phase_imag)
    real_high, real_low = split(real)
    imag_high, imag_low = split(imag)
    return signed_block(real_high, imag_high), signed_block(real_low, imag_low)


def wide_product(left_high, left_low, right_high, right_low):
    left = jnp.concatenate([left_high, left_high, left_low], axis=1)
    right = jnp.concatenate([right_high, right_low, right_high], axis=0)
    return dot(left, right)


def product(left_high, left_low, right_high, right_low):
    return dot(left_high, right_high) + dot(left_high, right_low) + dot(left_low, right_high)


def hbm(array):
    return pltpu.with_memory_space_constraint(array, pltpu.HBM)


def any_space():
    return pl.BlockSpec(memory_space=pl.ANY)


def smem():
    return pl.BlockSpec(memory_space=pltpu.SMEM)


def vmem():
    return pl.BlockSpec(memory_space=pltpu.VMEM)


def cost(flops=1000):
    return pl.CostEstimate(flops=flops, bytes_accessed=1000, transcendentals=0)


def params():
    return pltpu.CompilerParams(vmem_limit_bytes=VMEM_BYTES)


def chosen_rows(steps, piece_rows, rows, layout_ref):
    me = lax.axis_index("hi")
    row_bits = rows.bit_length() - 1
    sub = lax.broadcasted_iota(jnp.int32, (8, 128), 0)
    inner = jnp.zeros((8, 128), jnp.int32)
    inner_bits = piece_rows.bit_length() - 1
    for k in range(inner_bits):
        place = jnp.left_shift(jnp.int32(1), layout_ref[k])
        if k < 3:
            inner = inner + ((sub >> k) & 1) * place
        else:
            inner = jnp.concatenate([inner, inner + place], axis=0)
    places = []
    for step in steps:
        block = me ^ step
        base = jnp.int32(0)
        for k in range(inner_bits, row_bits):
            base = base + jnp.left_shift((block >> (k - inner_bits)) & 1, layout_ref[k])
        places.append(inner + base)
    places = jnp.concatenate(places, axis=0)
    lane = lax.broadcasted_iota(jnp.int32, places.shape, 1)
    return jnp.concatenate(
        [
            jnp.where(places == lane + start, 1.0, 0.0).astype(BF16)
            for start in range(0, rows, 128)
        ],
        axis=1,
    )


def first_kernel(
    groups,
    piece_rows,
    col_bits,
    top_bit,
    amplitudes_hbm,
    gates_hbm,
    phases_hbm,
    angles_hbm,
    bits_hbm,
    coupled_hbm,
    layout_hbm,
    pair_hbm,
    *refs,
):
    (
        pairs_ref,
        *out_refs,
        amplitudes_ref,
        gates_ref,
        phases_ref,
        angles_ref,
        bits_ref,
        coupled_ref,
        layout_ref,
        pair_ref,
        small_sems,
        chunk_sems,
    ) = refs
    rows, cols = amplitudes_ref.shape[2:]
    row_bits = rows.bit_length() - 1
    small = [
        pltpu.make_async_copy(source, target, small_sems.at[i])
        for i, (source, target) in enumerate(
            (
                (phases_hbm, phases_ref),
                (angles_hbm, angles_ref),
                (bits_hbm, bits_ref),
                (coupled_hbm, coupled_ref),
                (layout_hbm, layout_ref),
                (pair_hbm, pair_ref),
            )
        )
    ]
    count = chunk_sems.shape[0]
    step = rows // count
    chunks = []
    for k in range(count):
        part = pl.ds(k * step, step)
        chunks.append(
            [
                pltpu.make_async_copy(
                    gates_hbm.at[0, 0, :, part], gates_ref.at[0, :, part], chunk_sems.at[k, 0]
                ),
                pltpu.make_async_copy(
                    gates_hbm.at[0, 1, :, part], gates_ref.at[1, :, part], chunk_sems.at[k, 1]
                ),
                pltpu.make_async_copy(
                    amplitudes_hbm.at[:, :, part], amplitudes_ref.at[:, :, part], chunk_sems.at[k, 2]
                ),
            ]
        )
    for copy in small:
        copy.start()
    for chunk in chunks:
        for copy in chunk:
            copy.start()
    for copy in small:
        copy.wait()
    bit = (lax.axis_index("lo") >> top_bit) & 1
    c = pair_coefficients(pair_ref, 0, bit)
    for i in range(4):
        pairs_ref[i : i + 1, :] = jnp.full((1, cols), c[i], F32)
    pairs_ref[4:8, :] = jnp.zeros((4, cols), F32)
    cosine, sine = qubit_factors(0, phases_ref, bits_ref, coupled_ref)
    base_real, base_imag = sincos(angles_ref[0:1, 0:1])
    phase_real, phase_imag = row_phases(cosine, sine, col_bits, row_bits, base_real, base_imag)
    steps = [d for group in groups for d in group]
    chosen = chosen_rows(steps, piece_rows, rows, layout_ref)
    gated = None
    for k in range(count):
        for copy in chunks[k]:
            copy.wait()
        part = slice(k * step, (k + 1) * step)
        real_high, real_low = split(gates_ref[0, :, part])
        imag_high, imag_low = split(gates_ref[1, :, part])
        right_high, right_low = turned_rows(
            amplitudes_ref[0, 0, part], amplitudes_ref[1, 0, part], phase_real[part], phase_imag[part]
        )
        term = product(
            jnp.concatenate([real_high, imag_high], axis=1),
            jnp.concatenate([real_low, imag_low], axis=1),
            right_high,
            right_low,
        )
        gated = term if gated is None else gated + term
    gated_high, gated_low = split(gated)
    out = dot(chosen, gated_high) + dot(chosen, gated_low)
    start = 0
    for group, out_ref in zip(groups, out_refs, strict=True):
        size = len(group) * piece_rows
        out_ref[0] = out[start : start + size, :cols]
        out_ref[1] = out[start : start + size, cols:]
        start += size


def first(
    groups, piece_rows, col_bits, top_bit, amplitudes, gates, phases, angles, bits, coupled, layout, pair
):
    rows, cols = amplitudes.shape[2:]
    shapes = [jax.ShapeDtypeStruct((8, cols), F32)]
    shapes += [jax.ShapeDtypeStruct((2, len(group) * piece_rows, cols), F32) for group in groups]
    sources = (amplitudes, gates, phases, angles, bits, coupled, layout, pair)
    return pl.pallas_call(
        functools.partial(first_kernel, groups, piece_rows, col_bits, top_bit),
        out_shape=shapes,
        in_specs=[any_space()] * len(sources),
        out_specs=[vmem()] * len(shapes),
        scratch_shapes=[
            pltpu.VMEM(amplitudes.shape, F32),
            pltpu.VMEM(gates.shape[1:], F32),
            pltpu.VMEM(phases.shape, F32),
            pltpu.VMEM(angles.shape, F32),
            pltpu.SMEM(bits.shape, jnp.int32),
            pltpu.SMEM(coupled.shape, jnp.int32),
            pltpu.SMEM(layout.shape, jnp.int32),
            pltpu.SMEM(pair.shape, F32),
            pltpu.SemaphoreType.DMA((6,)),
            pltpu.SemaphoreType.DMA((CHUNKS, 3)),
        ],
        compiler_params=params(),
        cost_estimate=cost(),
        name="first",
    )(*[hbm(source) for source in sources])


def own_order(tile, piece_rows, me):
    lane = lax.broadcasted_iota(jnp.int32, tile.shape, 1)
    width = tile.shape[1]
    size = piece_rows
    bit = 0
    while size < width:
        upper = (lane & size) != 0
        swapped = jnp.where(
            upper, pltpu.roll(tile, size, 1), pltpu.roll(tile, width - size, 1)
        )
        tile = jnp.where(((me >> bit) & 1) == 1, swapped, tile)
        size *= 2
        bit += 1
    return tile


def phases_kernel(
    sets, piece_rows, col_bits, phases_ref, angles_ref, bits_ref, coupled_ref, pair_ref, *refs
):
    *out_refs, coefficients_ref, phase_real_ref, phase_imag_ref = refs
    me = lax.axis_index("hi")
    rows = phase_real_ref.shape[0]
    cols = coefficients_ref.shape[1]
    row_bits = rows.bit_length() - 1
    bit = lax.axis_index("lo") & 1
    before = qubit_factors(0, phases_ref, bits_ref, coupled_ref)
    after = qubit_factors(1, phases_ref, bits_ref, coupled_ref)
    base_real, base_imag = sincos(angles_ref[0:1, 1:2])
    phase_real_ref[...], phase_imag_ref[...] = row_phases(
        *after, col_bits, row_bits, base_real, base_imag
    )
    phase_real, phase_imag = turn(
        *col_phases(*before, col_bits, cols), *col_phases(*after, col_bits, cols)
    )
    c = pair_coefficients(pair_ref, 1, bit)
    c = turn(phase_real, phase_imag, c[0], c[1]) + turn(phase_real, phase_imag, c[2], c[3])
    for i in range(4):
        coefficients_ref[i : i + 1, :] = c[i]
    coefficients_ref[4:8, :] = jnp.zeros((4, cols), F32)
    for k, steps in enumerate(sets):
        for j, d in enumerate(steps):
            start = pl.multiple_of((me ^ d) * piece_rows, piece_rows)
            target = slice(j * piece_rows, (j + 1) * piece_rows)
            out_refs[2 * k][target, :] = phase_real_ref[pl.ds(start, piece_rows), :]
            out_refs[2 * k + 1][target, :] = phase_imag_ref[pl.ds(start, piece_rows), :]


def second_phases(sets, piece_rows, rows, col_bits, phases, angles, bits, coupled, pair):
    cols = 1 << col_bits
    shapes = []
    for steps in sets:
        shapes += [jax.ShapeDtypeStruct((len(steps) * piece_rows, 128), F32)] * 2
    shapes.append(jax.ShapeDtypeStruct((8, cols), F32))
    return pl.pallas_call(
        functools.partial(phases_kernel, sets, piece_rows, col_bits),
        out_shape=shapes,
        in_specs=[vmem(), vmem(), smem(), smem(), smem()],
        out_specs=[vmem()] * len(shapes),
        scratch_shapes=[pltpu.VMEM((rows, 128), F32)] * 2,
        compiler_params=params(),
        cost_estimate=cost(),
        name="second_phases",
    )(phases, angles, bits, coupled, pair)


def gates_kernel(sets, piece_rows, gates_hbm, *refs):
    *out_refs, gates_ref, sem = refs
    copy = pltpu.make_async_copy(gates_hbm.at[1], gates_ref, sem)
    copy.start()
    me = lax.axis_index("hi")
    size = gates_ref.shape[1] // 4
    quarter = size // piece_rows
    copy.wait()
    high, low = [], []
    for i in range(2):
        high_tiles, low_tiles = [], []
        for q in range(4):
            start = pl.multiple_of(((me // quarter) ^ q) * size, size)
            tile = own_order(gates_ref[i, :, pl.ds(start, size)], piece_rows, me)
            for tiles, part in zip((high_tiles, low_tiles), split(tile), strict=True):
                tiles.append(part)
        high.append(jnp.concatenate(high_tiles, axis=1))
        low.append(jnp.concatenate(low_tiles, axis=1))
    for k, steps in enumerate(sets):
        for part, out_ref in zip((high, low), out_refs[2 * k : 2 * k + 2], strict=True):
            out_ref[...] = jnp.concatenate(
                [
                    part[i][:, d * piece_rows : (d + 1) * piece_rows]
                    for i in range(2)
                    for d in steps
                ],
                axis=1,
            )


def second_gates(sets, piece_rows, gates):
    rows = gates.shape[2]
    shapes = []
    for steps in sets:
        shapes += [jax.ShapeDtypeStruct((rows, 2 * len(steps) * piece_rows), BF16)] * 2
    return pl.pallas_call(
        functools.partial(gates_kernel, sets, piece_rows),
        out_shape=shapes,
        in_specs=[any_space()],
        out_specs=[vmem()] * len(shapes),
        scratch_shapes=[pltpu.VMEM(gates.shape[1:], F32), pltpu.SemaphoreType.DMA],
        compiler_params=params(),
        cost_estimate=cost(),
        name="second_gates",
    )(hbm(gates))


def pair_coefficients(pair_ref, layer, bit):
    own = bit
    other = 1 - bit
    return (
        pair_ref[layer, 0, own, own],
        pair_ref[layer, 1, own, own],
        pair_ref[layer, 0, own, other],
        pair_ref[layer, 1, own, other],
    )


def combined(own, other, c):
    own_real, own_imag = turn(own[0], own[1], c[0], c[1])
    other_real, other_imag = turn(other[0], other[1], c[2], c[3])
    return own_real + other_real, own_imag + other_imag


def vector_coefficients(ref):
    return [ref[i : i + 1, :] for i in range(4)]


def combine_kernel(pairs_ref, own_ref, other_ref, *out_refs):
    c = vector_coefficients(pairs_ref)
    size = out_refs[0].shape[1]
    for i, out_ref in enumerate(out_refs):
        rows = slice(i * size, (i + 1) * size)
        out_ref[0], out_ref[1] = combined(
            (own_ref[0, rows], own_ref[1, rows]), (other_ref[0, rows], other_ref[1, rows]), c
        )


def combine(count, own, other, pairs, flops):
    shape = (2, own.shape[1] // count, own.shape[2])
    return pl.pallas_call(
        combine_kernel,
        out_shape=[jax.ShapeDtypeStruct(shape, F32)] * count,
        in_specs=[vmem()] * 3,
        out_specs=[vmem()] * count,
        compiler_params=params(),
        cost_estimate=cost(flops),
        name="combine",
    )(pairs, own, other)


def late_kernel(*refs):
    *part_refs, out_ref = refs
    size = part_refs[0].shape[1]
    for i, part_ref in enumerate(part_refs):
        out_ref[:, i * size : (i + 1) * size, :] = part_ref[...]


def joined(arrays, flops):
    _, size, cols = arrays[0].shape
    return pl.pallas_call(
        late_kernel,
        out_shape=jax.ShapeDtypeStruct((2, size * len(arrays), cols), F32),
        in_specs=[vmem()] * len(arrays),
        out_specs=vmem(),
        compiler_params=params(),
        cost_estimate=cost(flops),
        name="joined",
    )(*arrays)


def turned_pieces_kernel(phase_real_ref, phase_imag_ref, *refs):
    *piece_refs, out_ref = refs
    reps = out_ref.shape[2] // phase_real_ref.shape[1]
    start = 0
    for ref in piece_refs:
        part = slice(start, start + ref.shape[1])
        cosine = jnp.concatenate([phase_real_ref[part, :]] * reps, axis=1)
        sine = jnp.concatenate([phase_imag_ref[part, :]] * reps, axis=1)
        out_ref[0, part], out_ref[1, part] = turn(ref[0], ref[1], cosine, sine)
        start += ref.shape[1]


def turned_pieces(phase_parts, arrays):
    shape = (2, sum(a.shape[1] for a in arrays), arrays[0].shape[2])
    return pl.pallas_call(
        turned_pieces_kernel,
        out_shape=jax.ShapeDtypeStruct(shape, F32),
        in_specs=[vmem()] * (2 + len(arrays)),
        out_specs=vmem(),
        compiler_params=params(),
        cost_estimate=cost(MIDDLE_COST),
        name="turned_pieces",
    )(*phase_parts, *arrays)


def mixed_parts(coefficients_ref, own_ref, other_ref):
    c = vector_coefficients(coefficients_ref)
    real, imag = combined(own_ref, other_ref, c)
    real_high, real_low = split(real)
    imag_high, imag_low = split(imag)
    return signed_block(real_high, imag_high), signed_block(real_low, imag_low)


def middle_kernel(high_ref, low_ref, coefficients_ref, own_ref, other_ref, out_ref):
    cols = out_ref.shape[2]
    right_high, right_low = mixed_parts(coefficients_ref, own_ref, other_ref)
    out = wide_product(high_ref[...], low_ref[...], right_high, right_low)
    out_ref[0] = out[:, :cols]
    out_ref[1] = out[:, cols:]


def middle(parts, coefficients, own, other):
    return pl.pallas_call(
        middle_kernel,
        out_shape=jax.ShapeDtypeStruct((2, parts[0].shape[0], own.shape[2]), F32),
        in_specs=[vmem()] * 5,
        out_specs=vmem(),
        compiler_params=params(),
        cost_estimate=cost(),
        name="middle",
    )(*parts, coefficients, own, other)


def turned_kernel(
    phase_real_ref, phase_imag_ref, pairs_ref, own_ref, other_ref, last_ref, out_ref
):
    size = own_ref.shape[1]
    parts = (
        (slice(0, size), combined(own_ref, other_ref, vector_coefficients(pairs_ref))),
        (slice(size, out_ref.shape[1]), (last_ref[0], last_ref[1])),
    )
    reps = out_ref.shape[2] // phase_real_ref.shape[1]
    for part, (real, imag) in parts:
        cosine = jnp.concatenate([phase_real_ref[part, :]] * reps, axis=1)
        sine = jnp.concatenate([phase_imag_ref[part, :]] * reps, axis=1)
        out_ref[0, part], out_ref[1, part] = turn(real, imag, cosine, sine)


def turned(phase_parts, pairs, own, other, last):
    shape = (2, own.shape[1] + last.shape[1], own.shape[2])
    return pl.pallas_call(
        turned_kernel,
        out_shape=jax.ShapeDtypeStruct(shape, F32),
        in_specs=[vmem()] * 6,
        out_specs=vmem(),
        compiler_params=params(),
        cost_estimate=cost(),
        name="turned",
    )(*phase_parts, pairs, own, other, last)


def last_kernel(
    high_ref, low_ref, coefficients_ref, own_ref, other_ref, sum_ref, out_hbm, out_ref, sems
):
    cols = own_ref.shape[2]
    right_high, right_low = mixed_parts(coefficients_ref, own_ref, other_ref)
    unit = out_ref.shape[2] // sum(LAST_PARTS)
    copies = []
    start = 0
    for i, size in enumerate(LAST_PARTS):
        part = pl.ds(start, size * unit)
        start += size * unit
        out = wide_product(high_ref[part, :], low_ref[part, :], right_high, right_low)
        out_ref[0, 0, part] = sum_ref[0, part] + out[:, :cols]
        out_ref[1, 0, part] = sum_ref[1, part] + out[:, cols:]
        copies.append(
            pltpu.make_async_copy(
                out_ref.at[:, :, part], out_hbm.at[:, :, part], sems.at[i]
            )
        )
        copies[-1].start()
    for copy in copies:
        copy.wait()


def last(parts, coefficients, own, other, total):
    _, rows, cols = total.shape
    shape = (2, 1, rows, cols)
    return pl.pallas_call(
        last_kernel,
        out_shape=jax.ShapeDtypeStruct(shape, F32),
        in_specs=[vmem()] * 6,
        out_specs=any_space(),
        scratch_shapes=[pltpu.VMEM(shape, F32), pltpu.SemaphoreType.DMA((len(LAST_PARTS),))],
        compiler_params=params(),
        cost_estimate=cost(),
        name="last",
    )(*parts, coefficients, own, other, total)


def swap(value, axis, mask):
    return lax.ppermute(value, axis, [(i, i ^ mask) for i in range(lax.axis_size(axis))])


def after(value, earlier):
    return lax.optimization_barrier((value, earlier))[0]


def shards(amplitudes, gates, pair, angles, phases, bits, coupled, layout):
    rows = amplitudes.shape[2]
    cols = amplitudes.shape[3]
    col_bits = cols.bit_length() - 1
    count = lax.axis_size("hi")
    piece_rows = rows // count
    top_bit = lax.axis_size("lo").bit_length() - 2
    quarter = count // 4
    angles = angles.T
    beside = tuple(range(1, quarter))
    near = tuple(range(quarter, 2 * quarter))
    far = tuple(range(2 * quarter, 3 * quarter))
    early = tuple(reversed(range(3 * quarter, count)))
    late = far + beside
    cross = functools.partial(swap, axis="lo", mask=1 << top_bit)

    pairs, early_part, near_part, *late_parts = first(
        (early, (0,) + near) + tuple((d,) for d in late),
        piece_rows,
        col_bits,
        top_bit,
        amplitudes,
        gates,
        phases,
        angles,
        bits,
        coupled,
        layout,
        pair,
    )
    early_other = cross(early_part)
    late_parts = [swap(part, "hi", d) for part, d in zip(late_parts, late, strict=True)]
    near_other = cross(near_part)
    sets = ((0,) + near + early[:-1], late + early[-1:])
    *turns, coefficients = second_phases(
        sets, piece_rows, rows, col_bits, after(phases, early_part), angles, bits, coupled, pair
    )
    early_other = after(early_other, coefficients)
    early_parts = combine(len(early), early_part, early_other, pairs, COMBINE_COST)
    early_parts = [swap(part, "hi", d) for part, d in zip(early_parts, early, strict=True)]
    own_part, *near_parts = combine(1 + len(near), near_part, near_other, pairs, 1000)
    late_part = joined([after(part, own_part) for part in late_parts], LATE_COST)
    late_other = cross(late_part)
    near_parts = [swap(part, "hi", d) for part, d in zip(near_parts, near, strict=True)]
    half_part = joined(early_parts[:-1], HALF_COST)
    near_turned = turned_pieces(
        turns[:2], [own_part] + [after(part, half_part) for part in near_parts] + [half_part]
    )
    near_turned_other = swap(near_turned, "lo", 1)
    parts = second_gates(sets, piece_rows, after(gates, near_turned))
    late_turned = turned(
        turns[2:], pairs, late_part, after(late_other, parts[0]), early_parts[-1]
    )
    late_turned_other = swap(late_turned, "lo", 1)
    total = middle(parts[:2], coefficients, near_turned, near_turned_other)
    return last(parts[2:], coefficients, late_turned, late_turned_other, total)


def solution(mesh):
    placed = (
        P(None, ("hi", "lo"), None, None),
        P(),
        P(),
        P(None, ("hi", "lo")),
        P(),
        P(),
        P(),
        P(),
    )
    return jax.shard_map(
        shards,
        mesh=mesh,
        in_specs=placed,
        out_specs=P(None, ("hi", "lo"), None, None),
        check_vma=False,
    )
```
